512 devices in a mesh: ctx: 64 (over z, x), head: 8 (over y, core).
Axes of the slice: x: 4, y: 4, z: 16, core: 2. Of those that a mesh axis runs over, the one named last changes fastest.
Arguments:
- queries: bfloat16 [16384, 4096], P('ctx', 'head'), may hold values from -15 to 15
- key_rows: bfloat16 [16384, 4096], P('ctx', 'head'), may hold values from -4 to 4
- value_rows: bfloat16 [16384, 4096], P('ctx', 'head'), may hold values from -32 to 32
- cotangent: bfloat16 [16384, 4096], P('ctx', 'head'), may hold values from -6 to 6
- norm_gain: float32 [4096], P('head'), may hold values from 0.1 to 1.9
- pairing: int32 [64], replicated, may hold values from 0 to 63, as said below
Outputs:
- mixed: bfloat16 [16384, 4096], P('ctx', 'head')
- grad_query: bfloat16 [16384, 4096], P('ctx', 'head')
- grad_key: bfloat16 [16384, 4096], P('ctx', 'head')
- grad_value: bfloat16 [16384, 4096], P('ctx', 'head')
The draws below stay inside these ranges and needn't reach their ends.
Inputs may be any that keep to these rules, and one draw needn't show every extreme that they name: pairing is a permutation of the 64 blocks, and pairing[b] differs from b.
All inputs are finite; a program needn't handle non-finite values.
Results may differ from the reference program's by a relative error of at most 0.012.
Values may be sent and summed in bfloat16 or wider, within the bound.
A program may use at most 64 MiB of HBM per device.

```python
import math
import jax
import jax.numpy as jnp
from jax import lax

H = 32
HD = 128
BLOCK = 256
BLK_DEV = 1
BLOCKS = 64
TOKENS = 16384


def query_key_pair(base):
    folded = jax.random.fold_in(base, 11)
    streams = jax.random.split(folded, 2)
    width = H * HD
    drawn_query = jnp.clip(jax.random.normal(streams[0], (TOKENS, width), jnp.float32), -4.0, 4.0) * 2.0
    drawn_key = jnp.clip(jax.random.normal(streams[1], (TOKENS, width), jnp.float32), -4.0, 4.0)
    return (drawn_query, drawn_key)


def draw_queries(key, part):
    return query_key_pair(key)[0].astype(jnp.bfloat16)


def draw_key_rows(key, part):
    return query_key_pair(key)[1].astype(jnp.bfloat16)


def draw_value_rows(key, part):
    width = H * HD
    folded = jax.random.fold_in(key, 23)
    heads_of = (jnp.arange(width) // HD).astype(jnp.float32) / (H - 1)
    column_scale = 3.0 ** heads_of
    base_values = jnp.clip(jax.random.normal(folded, (TOKENS, width), jnp.float32), -4.0, 4.0)
    return (2.0 * base_values * column_scale[None, :]).astype(jnp.bfloat16)


def draw_pairing(key, part):
    devices = BLOCKS // BLK_DEV
    folded = jax.random.fold_in(key, 5)
    streams = jax.random.split(folded, BLK_DEV + 1)
    targets = []
    for column in range(BLK_DEV):
        cycle = jax.random.permutation(streams[column], devices).astype(jnp.int32)
        follow = jnp.zeros((devices,), jnp.int32).at[cycle].set(jnp.roll(cycle, -1))
        targets.append(follow)
    target = jnp.stack(targets, axis=1)
    ranking = jax.random.randint(streams[BLK_DEV], (devices, BLK_DEV), 0, 1 << 20) * BLK_DEV + jnp.arange(BLK_DEV, dtype=jnp.int32)[None, :]
    slots = jnp.argsort(ranking, axis=1).astype(jnp.int32)
    column_ids = jnp.broadcast_to(jnp.arange(BLK_DEV, dtype=jnp.int32)[None, :], (devices, BLK_DEV))
    landing = slots[target, column_ids]
    return (target * BLK_DEV + landing).reshape(-1).astype(jnp.int32)


def block_scale(stream_key, shape, pieces, least, largest):
    def one(dim, shards_of):
        draws = jax.random.uniform(jax.random.fold_in(jax.random.fold_in(stream_key, 6), dim), (shards_of,), jnp.float32, least / len(pieces), largest / len(pieces))
        return jnp.repeat(jnp.exp(draws), shape[dim] // shards_of).reshape((-1,) + (1,) * (len(shape) - dim - 1))

    gain = one(*pieces[0])
    for cut in pieces[1:]:
        gain = gain * one(*cut)
    return gain


def scatter_about(rng, shape, scale, limit, pieces=(), held_as=jnp.bfloat16):
    entries = scale * jax.random.normal(rng, shape, jnp.float32)
    if pieces:
        entries = entries * block_scale(rng, shape, pieces, -0.22, 0.18)
    return jnp.clip(entries, -limit, limit).astype(held_as)


def setup_inputs(seed: int = 0) -> dict:
    splits = jax.random.split(jax.random.key(seed), 7)
    queries = draw_queries(jax.random.fold_in(splits[6], 71), 0)
    key_rows = draw_key_rows(jax.random.fold_in(splits[6], 71), 0)
    value_rows = draw_value_rows(jax.random.fold_in(splits[6], 71), 0)
    cotangent = scatter_about(splits[3], (TOKENS, H * HD), 1.0, 6.0, ((0, 64), (1, 8)))
    norm_gain = jnp.clip(1.0 + 0.18 * jax.random.normal(splits[4], (H * HD,), jnp.float32), 0.1, 1.9)
    pairing = draw_pairing(jax.random.fold_in(splits[6], 71), 0)
    return dict(queries=queries, key_rows=key_rows, value_rows=value_rows, cotangent=cotangent, norm_gain=norm_gain, pairing=pairing)


def reference(queries, key_rows, value_rows, cotangent, norm_gain, pairing):
    f32 = jnp.float32
    bf16 = jnp.bfloat16
    factor = 1.0 / math.sqrt(HD)
    query_blocks = queries.reshape(BLOCKS, BLOCK, H, HD)
    key_blocks = key_rows.reshape(BLOCKS, BLOCK, H, HD)
    value_blocks = value_rows.reshape(BLOCKS, BLOCK, H, HD)
    places = jnp.arange(BLOCK)
    causal = places[:, None] >= places[None, :]

    def window_of(block_id):
        partner = pairing[block_id]
        before = (block_id - 1) % BLOCKS
        keys_here = jnp.concatenate([key_blocks[before], key_blocks[block_id], key_blocks[partner]], axis=0)
        values_here = jnp.concatenate([value_blocks[before], value_blocks[block_id], value_blocks[partner]], axis=0)
        earlier = jnp.broadcast_to(block_id > 0, (BLOCK, BLOCK))
        allowed = jnp.concatenate([earlier, causal, jnp.ones((BLOCK, BLOCK), bool)], axis=1)
        scores = jnp.einsum('ihd,jhd->hij', query_blocks[block_id].astype(f32), keys_here.astype(f32)) * factor
        scores = jnp.where(allowed[None], scores, -jnp.inf)
        return (keys_here, values_here, scores)

    def forward_block(block_id):
        keys_here, values_here, scores = window_of(block_id)
        highest = lax.optimization_barrier(jnp.max(scores, axis=-1, keepdims=True))
        logsum = highest + jnp.log(lax.optimization_barrier(jnp.sum(jnp.exp(scores - highest), axis=-1, keepdims=True)))
        weights = jnp.exp(scores - logsum)
        rounded = lax.optimization_barrier(weights.astype(bf16)).astype(f32)
        attn_block = jnp.einsum('hij,jhd->ihd', rounded, values_here.astype(f32)).astype(bf16)
        return (attn_block, logsum)
    block_ids = jnp.arange(BLOCKS, dtype=jnp.int32)
    attn, logsums = lax.map(forward_block, block_ids)
    attn_flat = attn.reshape(TOKENS, H * HD).astype(f32)
    rms_scale = lax.rsqrt(lax.optimization_barrier(jnp.mean(attn_flat * attn_flat, axis=1, keepdims=True)) + 1e-05)
    mixed = (attn_flat * rms_scale * norm_gain).astype(bf16)
    grad_in = norm_gain * cotangent.astype(f32)
    product_mean = lax.optimization_barrier(jnp.mean(grad_in * attn_flat, axis=1, keepdims=True))
    dattn = (rms_scale * grad_in - attn_flat * rms_scale ** 3 * product_mean).astype(bf16)
    dattn_blocks = dattn.reshape(BLOCKS, BLOCK, H, HD)
    delta = lax.optimization_barrier(jnp.sum(dattn_blocks.astype(f32) * attn.astype(f32), axis=-1))

    def backward_block(block_id):
        keys_here, values_here, scores = window_of(block_id)
        weights = jnp.exp(scores - logsums[block_id])
        rounded = lax.optimization_barrier(weights.astype(bf16)).astype(f32)
        grad_here = dattn_blocks[block_id].astype(f32)
        dprob = jnp.einsum('ihd,jhd->hij', grad_here, values_here.astype(f32))
        dscore = weights * (dprob - jnp.transpose(delta[block_id])[:, :, None])
        dscore = lax.optimization_barrier(dscore.astype(bf16)).astype(f32)
        dquery = (jnp.einsum('hij,jhd->ihd', dscore, keys_here.astype(f32)) * factor).astype(bf16)
        dkey = (jnp.einsum('hij,ihd->jhd', dscore, query_blocks[block_id].astype(f32)) * factor).astype(bf16)
        dvalue = jnp.einsum('hij,ihd->jhd', rounded, grad_here).astype(bf16)
        return (dquery, dkey, dvalue)
    grad_query, key_terms, value_terms = lax.map(backward_block, block_ids)

    def combine(terms):
        before_term = terms[:, :BLOCK]
        own_term = terms[:, BLOCK:2 * BLOCK]
        partner_term = terms[:, 2 * BLOCK:]
        from_next = jnp.roll(before_term, -1, axis=0)
        from_partner = jnp.zeros_like(partner_term).at[pairing].set(partner_term)
        total = own_term.astype(f32) + from_next.astype(f32) + from_partner.astype(f32)
        return total.astype(bf16).reshape(TOKENS, H * HD)
    return (mixed, grad_query.reshape(TOKENS, H * HD), combine(key_terms), combine(value_terms))
```

```python
import functools
import math

import jax
import jax.numpy as jnp
from jax import lax
from jax.experimental import pallas as pl
from jax.experimental.pallas import tpu as pltpu
from jax.sharding import PartitionSpec as P

HD = 128
ROWS = 16
EPSILON = 1e-05
MESH = pl.DeviceIdType.MESH
F32 = jnp.float32
BF16 = jnp.bfloat16


def mm(a, b, da, db):
    return lax.dot_general(a, b, (((da,), (db,)), ((), ())), preferred_element_type=F32)


def body(
    sizes,
    q_in,
    k_in,
    v_in,
    c_in,
    gain,
    pairing,
    inverse,
    mixed_out,
    gq_out,
    gk_out,
    gv_out,
    qh,
    kh,
    vh,
    ch,
    pk,
    pv,
    k1,
    v1,
    k2,
    v2,
    k3,
    v3,
    bkp,
    bvp,
    bkn,
    bvn,
    nk,
    nv,
    k4,
    v4,
    k5,
    v5,
    k6,
    v6,
    win,
    probs,
    dsc,
    acc,
    gin,
    att,
    dat,
    delta,
    stats,
    own_k,
    own_v,
    load_sem,
    send_sem,
    recv_sem,
):
    Z, X, G = sizes
    N = Z * X
    B = Z * ROWS
    factor = 1.0 / math.sqrt(HD)
    features = float(G * X * HD)
    ctx = lax.axis_index("ctx")
    hd = lax.axis_index("head")
    z = ctx // X
    x = lax.rem(ctx, X)
    mine = x * Z + z
    after = lax.rem(ctx + 1, N)
    before = lax.rem(ctx + N - 1, N)

    def peer(k):
        return lax.rem(z + k // X, Z) * X + lax.rem(x + k, X)

    def slot_of(j):
        return lax.rem(j, X) * Z + j // X

    def lanes(h):
        return pl.ds(pl.multiple_of(h * HD, HD), HD)

    def head_rows(h):
        return pl.ds(pl.multiple_of(h * Z, Z), Z)

    def block(ref, h):
        return ref[head_rows(h)].reshape(B, HD)

    def remote(src, dst, n, j, g):
        return pltpu.make_async_remote_copy(
            src_ref=src,
            dst_ref=dst,
            send_sem=send_sem.at[n],
            recv_sem=recv_sem.at[n],
            device_id=(j, g),
            device_id_type=MESH,
        )

    def loop(lo, hi, f):
        def step(k, carry):
            f(k)
            return carry

        lax.fori_loop(lo, hi, step, 0)

    def await_bytes(ref, sem):
        pltpu.make_async_copy(ref, ref, sem).wait()

    barrier = pltpu.get_barrier_semaphore()
    loop(
        1,
        N,
        lambda k: pl.semaphore_signal(
            barrier, inc=1, device_id=(peer(k), hd), device_id_type=MESH
        ),
    )
    loop(
        1,
        G,
        lambda k: pl.semaphore_signal(
            barrier, inc=1, device_id=(ctx, lax.rem(hd + k, G)), device_id_type=MESH
        ),
    )

    loads = []
    for n, (src, dst) in enumerate(((k_in, kh), (v_in, vh), (q_in, qh), (c_in, ch))):
        for h in range(X):
            copy = pltpu.make_async_copy(
                src.at[:, :, pl.ds(h * HD, HD)],
                dst.at[pl.ds(h * Z, Z)],
                load_sem.at[n * X + h],
            )
            copy.start()
            loads.append(copy)
    for copy in loads:
        copy.wait()
    k1[ctx] = kh[mine]
    v1[ctx] = vh[mine]
    pl.semaphore_wait(barrier, N - 1 + G - 1)

    loop(1, N, lambda k: remote(kh.at[slot_of(peer(k))], k1.at[ctx], 0, peer(k), hd).start())
    to_next_k = remote(kh, pk, 8, after, hd)
    to_next_k.start()
    loop(1, N, lambda k: remote(vh.at[slot_of(peer(k))], v1.at[ctx], 1, peer(k), hd).start())
    to_next_v = remote(vh, pv, 9, after, hd)
    to_next_v.start()

    def own_scores(h):
        s = mm(block(kh, h), block(qh, h), 1, 1) * factor
        key_at = lax.broadcasted_iota(jnp.int32, (B, B), 0)
        query_at = lax.broadcasted_iota(jnp.int32, (B, B), 1)
        win[h, pl.ds(B, B)] = jnp.where(key_at <= query_at, s, -jnp.inf)
        grad_in = block(ch, h).astype(F32) * gain[:, lanes(h)]
        gin[h] = grad_in.T

    loop(0, X, own_scores)

    def choose(dst, src, table):
        def f(j):
            dst[j] = src[table[j]]

        loop(0, N, f)

    def forward(src, dst, n):
        dst[mine] = src[ctx]
        loop(1, N, lambda k: remote(src.at[peer(k)], dst.at[mine], n, peer(k), hd).start())

    def await_pieces(dst, n):
        await_bytes(dst.at[pl.ds(0, N - 1)], recv_sem.at[n])

    await_pieces(k1, 0)
    choose(k2, k1, pairing)
    forward(k2, k3, 2)
    await_pieces(v1, 1)
    choose(v2, v1, pairing)
    forward(v2, v3, 3)

    to_next_k.wait_recv()

    def prior_scores(h):
        s = mm(block(pk, h), block(qh, h), 1, 1) * factor
        win[h, pl.ds(0, B)] = jnp.where(ctx > 0, s, -jnp.inf)

    loop(0, X, prior_scores)
    to_next_v.wait_recv()
    await_pieces(k3, 2)

    def softmax(h):
        win[h, pl.ds(2 * B, B)] = mm(block(k3, h), block(qh, h), 1, 1) * factor
        s = win[h]
        highest = jnp.max(s, axis=0, keepdims=True)
        logsum = highest + jnp.log(jnp.sum(jnp.exp(s - highest), axis=0, keepdims=True))
        w = jnp.exp(s - logsum)
        win[h] = w
        p = w.astype(BF16)
        probs[h] = p
        acc[h] = mm(block(pv, h), p[0:B], 0, 0) + mm(block(vh, h), p[B : 2 * B], 0, 0)

    loop(0, X, softmax)
    await_pieces(v3, 3)

    stats[hd] = jnp.zeros((8, B), F32)

    def attend(h):
        o = acc[h] + mm(block(v3, h), probs[h, pl.ds(2 * B, B)], 0, 0)
        a = o.astype(BF16).astype(F32)
        att[h] = a
        stats[hd, 0:1] += jnp.sum(a * a, axis=0, keepdims=True)
        stats[hd, 1:2] += jnp.sum(gin[h] * a, axis=0, keepdims=True)

    loop(0, X, attend)
    loop(
        1,
        G,
        lambda k: remote(stats.at[hd], stats.at[hd], 10, ctx, lax.rem(hd + k, G)).start(),
    )
    await_bytes(stats.at[pl.ds(0, G - 1)], recv_sem.at[10])
    total = jnp.sum(stats[...], axis=0)
    rms = lax.rsqrt(total[0:1] / features + EPSILON)
    slope = rms * rms * rms * (total[1:2] / features)

    def value_terms(k):
        h = lax.rem(x + k, X)
        a = att[h]
        d = (rms * gin[h] - a * slope).astype(BF16)
        dat[h] = d
        delta[h] = jnp.sum(d.astype(F32) * a, axis=0, keepdims=True)
        term = mm(probs[h, pl.ds(2 * B, B)], d, 1, 1).astype(BF16)
        bvp[head_rows(h)] = term.reshape(Z, ROWS, HD)

        def send(n):
            zj = lax.rem(z + n, Z)
            j = zj * X + h

            @pl.when(j != ctx)
            def _():
                remote(bvp.at[h * Z + zj], v4.at[ctx], 5, j, hd).start()

        loop(0, Z, send)

    loop(0, X, value_terms)
    v4[ctx] = bvp[mine]

    def score_grad(h, g, values):
        dp = mm(values, dat[h], 1, 0)
        d = (win[h, pl.ds(g * B, B)] * (dp - delta[h])).astype(BF16)
        dsc[h, pl.ds(g * B, B)] = d
        return d

    def key_terms(k):
        h = lax.rem(x + k, X)
        d = score_grad(h, 2, block(v3, h))
        term = (mm(d, block(qh, h), 1, 0) * factor).astype(BF16)
        bkp[head_rows(h)] = term.reshape(Z, ROWS, HD)

        def send(n):
            zj = lax.rem(z + n, Z)
            j = zj * X + h

            @pl.when(j != ctx)
            def _():
                remote(bkp.at[h * Z + zj], k4.at[ctx], 4, j, hd).start()

        loop(0, Z, send)

    loop(0, X, key_terms)
    k4[ctx] = bkp[mine]

    def prior_terms(h):
        d = score_grad(h, 0, block(pv, h))
        term = (mm(d, block(qh, h), 1, 0) * factor).astype(BF16)
        bkn[head_rows(h)] = term.reshape(Z, ROWS, HD)
        term = mm(probs[h, pl.ds(0, B)], dat[h], 1, 1).astype(BF16)
        bvn[head_rows(h)] = term.reshape(Z, ROWS, HD)

    loop(0, X, prior_terms)
    to_prior_v = remote(bvn, nv, 11, before, hd)
    to_prior_v.start()
    to_prior_k = remote(bkn, nk, 12, before, hd)
    to_prior_k.start()

    def own_terms(h):
        d = score_grad(h, 1, block(vh, h))
        own_k[h] = (mm(d, block(qh, h), 1, 0) * factor).astype(BF16).astype(F32)
        own_v[h] = mm(probs[h, pl.ds(B, B)], dat[h], 1, 1).astype(BF16).astype(F32)
        gq = (
            mm(dsc[h, pl.ds(0, B)], block(pk, h), 0, 0)
            + mm(dsc[h, pl.ds(B, B)], block(kh, h), 0, 0)
            + mm(dsc[h, pl.ds(2 * B, B)], block(k3, h), 0, 0)
        )
        gq_out[:, lanes(h)] = (gq * factor).astype(BF16)
        mixed_out[:, lanes(h)] = ((att[h] * rms).T * gain[:, lanes(h)]).astype(BF16)

    loop(0, X, own_terms)

    await_pieces(v4, 5)
    choose(v5, v4, inverse)
    forward(v5, v6, 7)
    await_pieces(k4, 4)
    choose(k5, k4, inverse)
    forward(k5, k6, 6)

    to_prior_v.wait_recv()
    to_prior_k.wait_recv()

    def add_next(h):
        own_v[h] += block(nv, h).astype(F32)
        own_k[h] += block(nk, h).astype(F32)

    loop(0, X, add_next)
    await_pieces(v6, 7)

    def give_v(h):
        gv_out[:, lanes(h)] = (own_v[h] + block(v6, h).astype(F32)).astype(BF16)

    loop(0, X, give_v)
    await_pieces(k6, 6)

    def give_k(h):
        gk_out[:, lanes(h)] = (own_k[h] + block(k6, h).astype(F32)).astype(BF16)

    loop(0, X, give_k)

    for n in range(8):
        await_bytes(k1.at[pl.ds(0, N - 1)], send_sem.at[n])
    await_bytes(stats.at[pl.ds(0, G - 1)], send_sem.at[10])
    for copy in (to_next_k, to_next_v, to_prior_v, to_prior_k):
        copy.wait_send()


def on_device(sizes, queries, key_rows, value_rows, cotangent, norm_gain, pairing):
    Z, X, G = sizes
    N, B, W = Z * X, Z * ROWS, X * HD
    tiles = (Z, ROWS, W)
    places = jnp.arange(N, dtype=jnp.int32)
    inverse = jnp.sum(
        jnp.where(pairing[None, :] == places[:, None], places[None, :], 0), axis=1
    ).astype(jnp.int32)
    vmem = pl.BlockSpec(memory_space=pltpu.VMEM)
    smem = pl.BlockSpec(memory_space=pltpu.SMEM)
    hbm = pl.BlockSpec(memory_space=pl.ANY)
    pieces = pltpu.VMEM((N, ROWS, HD), BF16)
    square = pltpu.VMEM((X, HD, B), F32)
    out = jax.ShapeDtypeStruct((B, W), BF16)
    return pl.pallas_call(
        functools.partial(body, sizes),
        out_shape=(out,) * 4,
        in_specs=[hbm] * 4 + [vmem, smem, smem],
        out_specs=(vmem,) * 4,
        scratch_shapes=[pieces] * 24
        + [
            pltpu.VMEM((X, 3 * B, B), F32),
            pltpu.VMEM((X, 3 * B, B), BF16),
            pltpu.VMEM((X, 3 * B, B), BF16),
            square,
            square,
            square,
            pltpu.VMEM((X, HD, B), BF16),
            pltpu.VMEM((X, 1, B), F32),
            pltpu.VMEM((G, 8, B), F32),
            pltpu.VMEM((X, B, HD), F32),
            pltpu.VMEM((X, B, HD), F32),
            pltpu.SemaphoreType.DMA((4 * X,)),
            pltpu.SemaphoreType.DMA((13,)),
            pltpu.SemaphoreType.DMA((13,)),
        ],
        compiler_params=pltpu.CompilerParams(
            collective_id=0, has_side_effects=True, vmem_limit_bytes=48 << 20
        ),
    )(
        queries.reshape(tiles),
        key_rows.reshape(tiles),
        value_rows.reshape(tiles),
        cotangent.reshape(tiles),
        norm_gain.reshape(1, W),
        pairing,
        inverse,
    )


def solution(mesh):
    heads_here = 4
    sizes = (mesh.shape["ctx"] // heads_here, heads_here, mesh.shape["head"])
    spec = P("ctx", "head")
    return jax.shard_map(
        functools.partial(on_device, sizes),
        mesh=mesh,
        in_specs=(spec, spec, spec, spec, P("head"), P()),
        out_specs=(spec,) * 4,
        check_vma=False,
    )
```

```python
import functools
import math

import jax
import jax.numpy as jnp
from jax import lax
from jax.experimental import pallas as pl
from jax.experimental.pallas import tpu as pltpu
from jax.sharding import PartitionSpec as P

HD = 128
ROWS = 16
EPSILON = 1e-05
MESH = pl.DeviceIdType.MESH
F32 = jnp.float32
BF16 = jnp.bfloat16


def mm(a, b, da, db):
    return lax.dot_general(a, b, (((da,), (db,)), ((), ())), preferred_element_type=F32)


def body(
    sizes,
    q_in,
    k_in,
    v_in,
    c_in,
    gain_in,
    pairing_in,
    mixed_out,
    gq_out,
    gk_out,
    gv_out,
    qh,
    kh,
    vh,
    ch,
    pk,
    pv,
    k1,
    v1,
    k2,
    v2,
    k3,
    v3,
    bkp,
    bvp,
    bkn,
    bvn,
    nk,
    nv,
    k4,
    v4,
    k5,
    v5,
    k6,
    v6,
    win,
    probs,
    dsc,
    acc,
    gin,
    att,
    dat,
    delta,
    stats,
    own_k,
    own_v,
    rk,
    rv,
    rkb,
    rvb,
    gain,
    pair_row,
    inverse_row,
    pairing,
    inverse,
    load_sem,
    send_sem,
    recv_sem,
):
    Z, X, G = sizes
    N = Z * X
    B = Z * ROWS
    factor = 1.0 / math.sqrt(HD)
    features = float(G * X * HD)
    ctx = lax.axis_index("ctx")
    hd = lax.axis_index("head")
    z = ctx // X
    x = lax.rem(ctx, X)
    mine = x * Z + z
    after = lax.rem(ctx + 1, N)
    before = lax.rem(ctx + N - 1, N)

    def peer(k):
        return lax.rem(z + k // X, Z) * X + lax.rem(x + k, X)

    def slot_of(j):
        return lax.rem(j, X) * Z + j // X

    def lanes(h):
        return pl.ds(pl.multiple_of(h * HD, HD), HD)

    def head_rows(h):
        return pl.ds(pl.multiple_of(h * Z, Z), Z)

    def block(ref, h):
        return ref[head_rows(h)].reshape(B, HD)

    def remote(src, dst, n, j, g, m=None):
        return pltpu.make_async_remote_copy(
            src_ref=src,
            dst_ref=dst,
            send_sem=send_sem.at[n],
            recv_sem=recv_sem.at[n if m is None else m],
            device_id=(j, g),
            device_id_type=MESH,
        )

    def loop(lo, hi, f):
        def step(k, carry):
            f(k)
            return carry

        lax.fori_loop(lo, hi, step, 0)

    def await_bytes(ref, sem):
        pltpu.make_async_copy(ref, ref, sem).wait()

    barrier = pltpu.get_barrier_semaphore()
    loop(
        1,
        N,
        lambda k: pl.semaphore_signal(
            barrier, inc=1, device_id=(peer(k), hd), device_id_type=MESH
        ),
    )
    loop(
        1,
        G,
        lambda k: pl.semaphore_signal(
            barrier, inc=1, device_id=(ctx, lax.rem(hd + k, G)), device_id_type=MESH
        ),
    )

    small = (
        pltpu.make_async_copy(gain_in, gain, load_sem.at[4 * X]),
        pltpu.make_async_copy(pairing_in, pair_row, load_sem.at[4 * X + 1]),
        pltpu.make_async_copy(pairing_in, pairing, load_sem.at[4 * X + 2]),
    )
    for copy in small:
        copy.start()
    loads = []
    for n, (src, dst) in enumerate(((k_in, kh), (v_in, vh), (q_in, qh), (c_in, ch))):
        for h in range(X):
            copy = pltpu.make_async_copy(
                src.at[:, :, pl.ds(h * HD, HD)],
                dst.at[pl.ds(h * Z, Z)],
                load_sem.at[n * X + h],
            )
            copy.start()
            loads.append(copy)
    for copy in small:
        copy.wait()
    down = lax.broadcasted_iota(jnp.int32, (N, N), 0)
    across = lax.broadcasted_iota(jnp.int32, (N, N), 1)
    partners = jnp.broadcast_to(pair_row[...], (N, N))
    partner_of = jnp.sum(jnp.where(down == across, partners, 0), axis=1, keepdims=True)
    inverse_row[...] = jnp.max(jnp.where(partner_of == across, down, 0), axis=0, keepdims=True)
    turn = pltpu.make_async_copy(inverse_row, inverse, load_sem.at[4 * X + 3])
    turn.start()
    for copy in loads:
        copy.wait()
    turn.wait()
    k1[ctx] = kh[mine]
    v1[ctx] = vh[mine]
    pl.semaphore_wait(barrier, N - 1 + G - 1)

    def pass_on(src, relay, dst, n, edge, step, target):
        @pl.when(x != edge)
        def _():
            remote(src, dst, n, target, hd).start()

        @pl.when(x == edge)
        def _():
            for h in range(1, X):
                via = edge + h * step
                part = pl.ds(via * Z, Z)
                remote(src.at[part], relay, n, z * X + via, hd, n + 2).start()
            part = pl.ds(edge * Z, Z)
            remote(src.at[part], dst.at[part], n, target, hd).start()

    def relay_on(relay, dst, n, edge, target):
        @pl.when(x != edge)
        def _():
            await_bytes(relay, recv_sem.at[n + 2])
            remote(relay, dst.at[head_rows(x)], n + 2, target, hd, n).start()

    def end_pass(src, relay, n, edge):
        await_bytes(src, send_sem.at[n])

        @pl.when(x != edge)
        def _():
            await_bytes(relay, send_sem.at[n + 2])

    over = lax.rem(z + 1, Z) * X
    under = lax.rem(z + Z - 1, Z) * X + X - 1

    loop(1, N, lambda k: remote(kh.at[slot_of(peer(k))], k1.at[ctx], 0, peer(k), hd).start())
    pass_on(kh, rk, pk, 8, X - 1, -1, after)
    loop(1, N, lambda k: remote(vh.at[slot_of(peer(k))], v1.at[ctx], 1, peer(k), hd).start())
    pass_on(vh, rv, pv, 9, X - 1, -1, after)

    def own_scores(h):
        s = mm(block(kh, h), block(qh, h), 1, 1) * factor
        key_at = lax.broadcasted_iota(jnp.int32, (B, B), 0)
        query_at = lax.broadcasted_iota(jnp.int32, (B, B), 1)
        win[h, pl.ds(B, B)] = jnp.where(key_at <= query_at, s, -jnp.inf)
        grad_in = block(ch, h).astype(F32) * gain[:, lanes(h)]
        gin[h] = grad_in.T

    loop(0, X, own_scores)

    def choose(dst, src, table):
        def f(j):
            dst[j] = src[table[0, j]]

        loop(0, N, f)

    def forward(src, dst, n):
        dst[mine] = src[ctx]
        loop(1, N, lambda k: remote(src.at[peer(k)], dst.at[mine], n, peer(k), hd).start())

    def await_pieces(dst, n):
        await_bytes(dst.at[pl.ds(0, N - 1)], recv_sem.at[n])

    await_pieces(k1, 0)
    choose(k2, k1, pairing)
    forward(k2, k3, 2)
    relay_on(rk, pk, 8, X - 1, over)
    await_pieces(v1, 1)
    choose(v2, v1, pairing)
    forward(v2, v3, 3)
    relay_on(rv, pv, 9, X - 1, over)

    await_bytes(pk, recv_sem.at[8])

    def prior_scores(h):
        s = mm(block(pk, h), block(qh, h), 1, 1) * factor
        win[h, pl.ds(0, B)] = jnp.where(ctx > 0, s, -jnp.inf)

    loop(0, X, prior_scores)
    await_bytes(pv, recv_sem.at[9])
    await_pieces(k3, 2)

    def softmax(h):
        win[h, pl.ds(2 * B, B)] = mm(block(k3, h), block(qh, h), 1, 1) * factor
        s = win[h]
        highest = jnp.max(s, axis=0, keepdims=True)
        logsum = highest + jnp.log(jnp.sum(jnp.exp(s - highest), axis=0, keepdims=True))
        w = jnp.exp(s - logsum)
        win[h] = w
        p = w.astype(BF16)
        probs[h] = p
        acc[h] = mm(block(pv, h), p[0:B], 0, 0) + mm(block(vh, h), p[B : 2 * B], 0, 0)

    loop(0, X, softmax)
    await_pieces(v3, 3)

    stats[hd] = jnp.zeros((8, B), F32)

    def attend(h):
        o = acc[h] + mm(block(v3, h), probs[h, pl.ds(2 * B, B)], 0, 0)
        a = o.astype(BF16).astype(F32)
        att[h] = a
        stats[hd, 0:1] += jnp.sum(a * a, axis=0, keepdims=True)
        stats[hd, 1:2] += jnp.sum(gin[h] * a, axis=0, keepdims=True)

    loop(0, X, attend)
    loop(
        1,
        G,
        lambda k: remote(stats.at[hd], stats.at[hd], 12, ctx, lax.rem(hd + k, G)).start(),
    )
    await_bytes(stats.at[pl.ds(0, G - 1)], recv_sem.at[12])
    total = jnp.sum(stats[...], axis=0)
    rms = lax.rsqrt(total[0:1] / features + EPSILON)
    slope = rms * rms * rms * (total[1:2] / features)

    def value_terms(k):
        h = lax.rem(x + k, X)
        a = att[h]
        d = (rms * gin[h] - a * slope).astype(BF16)
        dat[h] = d
        delta[h] = jnp.sum(d.astype(F32) * a, axis=0, keepdims=True)
        term = mm(probs[h, pl.ds(2 * B, B)], d, 1, 1).astype(BF16)
        bvp[head_rows(h)] = term.reshape(Z, ROWS, HD)

        def send(n):
            zj = lax.rem(z + n, Z)
            j = zj * X + h

            @pl.when(j != ctx)
            def _():
                remote(bvp.at[h * Z + zj], v4.at[ctx], 5, j, hd).start()

        loop(0, Z, send)

    loop(0, X, value_terms)
    v4[ctx] = bvp[mine]

    def score_grad(h, g, values):
        dp = mm(values, dat[h], 1, 0)
        d = (win[h, pl.ds(g * B, B)] * (dp - delta[h])).astype(BF16)
        dsc[h, pl.ds(g * B, B)] = d
        return d

    def key_terms(k):
        h = lax.rem(x + k, X)
        d = score_grad(h, 2, block(v3, h))
        term = (mm(d, block(qh, h), 1, 0) * factor).astype(BF16)
        bkp[head_rows(h)] = term.reshape(Z, ROWS, HD)

        def send(n):
            zj = lax.rem(z + n, Z)
            j = zj * X + h

            @pl.when(j != ctx)
            def _():
                remote(bkp.at[h * Z + zj], k4.at[ctx], 4, j, hd).start()

        loop(0, Z, send)

    loop(0, X, key_terms)
    k4[ctx] = bkp[mine]

    def prior_terms(h):
        d = score_grad(h, 0, block(pv, h))
        term = (mm(d, block(qh, h), 1, 0) * factor).astype(BF16)
        bkn[head_rows(h)] = term.reshape(Z, ROWS, HD)
        term = mm(probs[h, pl.ds(0, B)], dat[h], 1, 1).astype(BF16)
        bvn[head_rows(h)] = term.reshape(Z, ROWS, HD)

    loop(0, X, prior_terms)
    pass_on(bvn, rvb, nv, 13, 0, 1, before)
    pass_on(bkn, rkb, nk, 14, 0, 1, before)

    def own_terms(h):
        d = score_grad(h, 1, block(vh, h))
        own_k[h] = (mm(d, block(qh, h), 1, 0) * factor).astype(BF16).astype(F32)
        own_v[h] = mm(probs[h, pl.ds(B, B)], dat[h], 1, 1).astype(BF16).astype(F32)
        gq = (
            mm(dsc[h, pl.ds(0, B)], block(pk, h), 0, 0)
            + mm(dsc[h, pl.ds(B, B)], block(kh, h), 0, 0)
            + mm(dsc[h, pl.ds(2 * B, B)], block(k3, h), 0, 0)
        )
        gq_out[:, lanes(h)] = (gq * factor).astype(BF16)
        mixed_out[:, lanes(h)] = ((att[h] * rms).T * gain[:, lanes(h)]).astype(BF16)

    loop(0, X, own_terms)

    await_pieces(v4, 5)
    choose(v5, v4, inverse)
    forward(v5, v6, 7)
    relay_on(rvb, nv, 13, 0, under)
    relay_on(rkb, nk, 14, 0, under)
    await_pieces(k4, 4)
    choose(k5, k4, inverse)
    forward(k5, k6, 6)

    await_bytes(nv, recv_sem.at[13])
    await_bytes(nk, recv_sem.at[14])

    def add_next(h):
        own_v[h] += block(nv, h).astype(F32)
        own_k[h] += block(nk, h).astype(F32)

    loop(0, X, add_next)
    await_pieces(v6, 7)

    def give_v(h):
        gv_out[:, lanes(h)] = (own_v[h] + block(v6, h).astype(F32)).astype(BF16)

    loop(0, X, give_v)
    await_pieces(k6, 6)

    def give_k(h):
        gk_out[:, lanes(h)] = (own_k[h] + block(k6, h).astype(F32)).astype(BF16)

    loop(0, X, give_k)

    for n in range(8):
        await_bytes(k1.at[pl.ds(0, N - 1)], send_sem.at[n])
    await_bytes(stats.at[pl.ds(0, G - 1)], send_sem.at[12])
    end_pass(kh, rk, 8, X - 1)
    end_pass(vh, rv, 9, X - 1)
    end_pass(bvn, rvb, 13, 0)
    end_pass(bkn, rkb, 14, 0)


def write_out(*refs):
    sem = refs[8]
    copies = [pltpu.make_async_copy(refs[n], refs[4 + n], sem.at[n]) for n in range(4)]
    for copy in copies:
        copy.start()
    for copy in copies:
        copy.wait()


def on_device(sizes, queries, key_rows, value_rows, cotangent, norm_gain, pairing):
    Z, X, G = sizes
    N, B, W = Z * X, Z * ROWS, X * HD
    tiles = (Z, ROWS, W)
    vmem = pl.BlockSpec(memory_space=pltpu.VMEM)
    hbm = pl.BlockSpec(memory_space=pltpu.HBM)
    part = pltpu.VMEM((Z, ROWS, HD), BF16)
    pieces = pltpu.VMEM((N, ROWS, HD), BF16)
    square = pltpu.VMEM((X, HD, B), F32)
    out = jax.ShapeDtypeStruct((B, W), BF16)
    held = pl.pallas_call(
        functools.partial(body, sizes),
        out_shape=(out,) * 4,
        in_specs=[hbm] * 6,
        out_specs=(vmem,) * 4,
        scratch_shapes=[pieces] * 24
        + [
            pltpu.VMEM((X, 3 * B, B), F32),
            pltpu.VMEM((X, 3 * B, B), BF16),
            pltpu.VMEM((X, 3 * B, B), BF16),
            square,
            square,
            square,
            pltpu.VMEM((X, HD, B), BF16),
            pltpu.VMEM((X, 1, B), F32),
            pltpu.VMEM((G, 8, B), F32),
            pltpu.VMEM((X, B, HD), F32),
            pltpu.VMEM((X, B, HD), F32),
            part,
            part,
            part,
            part,
            pltpu.VMEM((1, W), F32),
            pltpu.VMEM((1, N), jnp.int32),
            pltpu.VMEM((1, N), jnp.int32),
            pltpu.SMEM((1, N), jnp.int32),
            pltpu.SMEM((1, N), jnp.int32),
            pltpu.SemaphoreType.DMA((4 * X + 4,)),
            pltpu.SemaphoreType.DMA((17,)),
            pltpu.SemaphoreType.DMA((17,)),
        ],
        compiler_params=pltpu.CompilerParams(
            collective_id=0, has_side_effects=True, vmem_limit_bytes=56 << 20
        ),
    )(
        queries.reshape(tiles),
        key_rows.reshape(tiles),
        value_rows.reshape(tiles),
        cotangent.reshape(tiles),
        norm_gain.reshape(1, W),
        pairing.reshape(1, N),
    )
    return pl.pallas_call(
        write_out,
        out_shape=(out,) * 4,
        in_specs=[vmem] * 4,
        out_specs=(hbm,) * 4,
        scratch_shapes=[pltpu.SemaphoreType.DMA((4,))],
    )(*held)


def solution(mesh):
    heads_here = 4
    sizes = (mesh.shape["ctx"] // heads_here, heads_here, mesh.shape["head"])
    spec = P("ctx", "head")
    return jax.shard_map(
        functools.partial(on_device, sizes),
        mesh=mesh,
        in_specs=(spec, spec, spec, spec, P("head"), P()),
        out_specs=(spec,) * 4,
        check_vma=False,
    )
```

```python
import functools
import math
import types

import jax
import jax.numpy as jnp
from jax import lax
from jax.experimental import pallas as pl
from jax.experimental.pallas import tpu as pltpu
from jax.sharding import PartitionSpec as P

HD = 128
ROWS = 16
EPSILON = 1e-05
MESH = pl.DeviceIdType.MESH
F32 = jnp.float32
BF16 = jnp.bfloat16

K_ONE, V_ONE, Q_ONE, D_ONE, K_TWO, V_TWO, Q_TWO, D_TWO = range(8)
PASS_K, PASS_V, RELAY_K, RELAY_V, BACK_V, BACK_K, RELAY_BV, RELAY_BK, STATS, E_ONE, E_TWO, HEAD = range(8, 20)


def mm(a, b, da, db):
    return lax.dot_general(a, b, (((da,), (db,)), ((), ())), preferred_element_type=F32)


def scratch(sizes):
    Z, X, G = sizes
    N, B, W = Z * X, Z * ROWS, X * HD
    pieces = pltpu.VMEM((N, ROWS, HD), BF16)
    part = pltpu.VMEM((Z, ROWS, HD), BF16)
    turned = pltpu.VMEM((X, HD, B), F32)
    upright = pltpu.VMEM((X, B, HD), F32)
    return dict(
        qh=pieces, kh=pieces, vh=pieces, ch=pieces,
        k1=pieces, v1=pieces, q1=pieces, d1=pieces,
        k2=pieces, v2=pieces, q2=pieces, d2=pieces,
        k3=pieces, v3=pieces, q3=pieces, d3=pieces,
        d0=pieces, pk=pieces, pv=pieces, bk=pieces, bv=pieces, nk=pieces, nv=pieces,
        rk=part, rv=part, rbk=part, rbv=part,
        win=pltpu.VMEM((X, 3 * B, B), F32),
        probs=pltpu.VMEM((X, 3 * B, B), BF16),
        dsc=pltpu.VMEM((X, 3 * B, B), BF16),
        win_in=pltpu.VMEM((X, B, B), F32),
        probs_in=pltpu.VMEM((X, B, B), BF16),
        acc=turned, gin=turned, att=turned,
        dat=pltpu.VMEM((X, HD, B), BF16),
        delta=pltpu.VMEM((X, 1, B), F32),
        lse=pltpu.VMEM((X, 1, B), F32),
        stats=pltpu.VMEM((G, 8, B), F32),
        e0=pltpu.VMEM((2 * X, 2, B // 2), F32),
        e1=pltpu.VMEM((N, 2, B // 2), F32),
        e2=pltpu.VMEM((N, 2, B // 2), F32),
        e3=pltpu.VMEM((2 * X, 2, B // 2), F32),
        own_k=upright, own_v=upright,
        gain=pltpu.VMEM((1, W), F32),
        pair_row=pltpu.VMEM((1, N), jnp.int32),
        inverse_row=pltpu.VMEM((1, N), jnp.int32),
        pairing=pltpu.SMEM((1, N), jnp.int32),
        inverse=pltpu.SMEM((1, N), jnp.int32),
        load_sem=pltpu.SemaphoreType.DMA((4 * X + 4,)),
        send_sem=pltpu.SemaphoreType.DMA((HEAD,)),
        recv_sem=pltpu.SemaphoreType.DMA((HEAD + X,)),
    )


def body(sizes, q_in, k_in, v_in, c_in, gain_in, pairing_in, mixed_out, gq_out, gk_out, gv_out, *refs):
    s = types.SimpleNamespace(**dict(zip(scratch(sizes), refs)))
    Z, X, G = sizes
    N = Z * X
    B = Z * ROWS
    half = B // 2
    factor = 1.0 / math.sqrt(HD)
    features = float(G * X * HD)
    ctx = lax.axis_index("ctx")
    hd = lax.axis_index("head")
    z = ctx // X
    x = lax.rem(ctx, X)

    def wrap(i, n):
        return jnp.where(i >= n, i - n, i)

    after = wrap(ctx + 1, N)
    before = wrap(ctx + N - 1, N)
    over = wrap(z + 1, Z) * X
    under = wrap(z + Z - 1, Z) * X + X - 1
    columns = [wrap(x + n, X) for n in range(X)]

    def via(h, zj):
        return zj * X + 2 * lax.rem(h, 2) + lax.rem(zj + h // 2, 2)

    my_head = 2 * lax.rem(x + z, 2) + x // 2
    mine = my_head * Z + z

    def lanes(h):
        return pl.ds(pl.multiple_of(h * HD, HD), HD)

    def head_rows(h):
        return pl.ds(pl.multiple_of(h * Z, Z), Z)

    def block(ref, h):
        return ref[head_rows(h)].reshape(B, HD)

    def remote(src, dst, n, j, g, m=None):
        return pltpu.make_async_remote_copy(
            src_ref=src,
            dst_ref=dst,
            send_sem=s.send_sem.at[n],
            recv_sem=s.recv_sem.at[n if m is None else m],
            device_id=(j, g),
            device_id_type=MESH,
        )

    def loop(lo, hi, f):
        def step(k, carry):
            f(k)
            return carry

        lax.fori_loop(lo, hi, step, 0)

    def each_peer(f):
        for n in range(1, X):
            f(z * X + columns[n])

        def along_z(k):
            zj = wrap(z + k, Z)
            for n in range(X):
                f(zj * X + columns[n])

        loop(1, Z, along_z)

    def each_head_peer(f):
        loop(1, G, lambda k: f(wrap(hd + k, G)))

    def await_bytes(ref, sem):
        pltpu.make_async_copy(ref, ref, sem).wait()

    barrier = pltpu.get_barrier_semaphore()
    each_peer(lambda j: pl.semaphore_signal(barrier, inc=1, device_id=(j, hd), device_id_type=MESH))
    each_head_peer(lambda g: pl.semaphore_signal(barrier, inc=1, device_id=(ctx, g), device_id_type=MESH))

    small = (
        pltpu.make_async_copy(pairing_in, s.pair_row, s.load_sem.at[4 * X + 1]),
        pltpu.make_async_copy(pairing_in, s.pairing, s.load_sem.at[4 * X + 2]),
        pltpu.make_async_copy(gain_in, s.gain, s.load_sem.at[4 * X]),
    )
    loads = []
    for n, (src, dst) in enumerate(((k_in, s.kh), (v_in, s.vh), (q_in, s.qh), (c_in, s.ch))):
        for h in range(X):
            loads.append(
                pltpu.make_async_copy(
                    src.at[:, :, pl.ds(h * HD, HD)], dst.at[pl.ds(h * Z, Z)], s.load_sem.at[n * X + h]
                )
            )
    for copy in loads[:X] + list(small) + loads[X:]:
        copy.start()
    for copy in small:
        copy.wait()
    down = lax.broadcasted_iota(jnp.int32, (N, N), 0)
    across = lax.broadcasted_iota(jnp.int32, (N, N), 1)
    partners = jnp.broadcast_to(s.pair_row[...], (N, N))
    partner_of = jnp.sum(jnp.where(down == across, partners, 0), axis=1, keepdims=True)
    s.inverse_row[...] = jnp.max(jnp.where(partner_of == across, down, 0), axis=0, keepdims=True)
    turn = pltpu.make_async_copy(s.inverse_row, s.inverse, s.load_sem.at[4 * X + 3])
    turn.start()
    for copy in loads:
        copy.wait()
    turn.wait()
    s.k1[ctx] = s.kh[mine]
    s.v1[ctx] = s.vh[mine]
    s.q1[ctx] = s.qh[mine]
    pl.semaphore_wait(barrier, N - 1 + G - 1)

    def pass_on(src, relay, dst, n, edge, step, target):
        @pl.when(x != edge)
        def _():
            remote(src, dst, n, target, hd).start()

        @pl.when(x == edge)
        def _():
            for h in range(1, X):
                by = edge + h * step
                part = pl.ds(by * Z, Z)
                remote(src.at[part], relay, n, z * X + by, hd, n + 2).start()
            part = pl.ds(edge * Z, Z)
            remote(src.at[part], dst.at[part], n, target, hd).start()

    def relay_on(relay, dst, n, edge, target):
        @pl.when(x != edge)
        def _():
            await_bytes(relay, s.recv_sem.at[n + 2])
            remote(relay, dst.at[head_rows(x)], n + 2, target, hd, n).start()

    def end_pass(src, relay, n, edge):
        await_bytes(src, s.send_sem.at[n])

        @pl.when(x != edge)
        def _():
            await_bytes(relay, s.send_sem.at[n + 2])

    def spread(src, dst, n):
        def of_head(h):
            def to(k):
                zj = wrap(z + k, Z)
                j = via(h, zj)

                @pl.when(j != ctx)
                def _():
                    remote(src.at[h * Z + zj], dst.at[ctx], n, j, hd).start()

            loop(0, Z, to)

        loop(0, X, of_head)

    def choose(dst, src, table):
        def f(j):
            dst[j] = src[table[0, j]]

        loop(0, N, f)

    def forward(src, dst, n):
        dst[mine] = src[ctx]
        each_peer(lambda j: remote(src.at[j], dst.at[mine], n, j, hd).start())

    def await_pieces(dst, n):
        await_bytes(dst.at[pl.ds(0, N - 1)], s.recv_sem.at[n])

    spread(s.kh, s.k1, K_ONE)
    pass_on(s.kh, s.rk, s.pk, PASS_K, X - 1, -1, after)
    spread(s.vh, s.v1, V_ONE)
    pass_on(s.vh, s.rv, s.pv, PASS_V, X - 1, -1, after)
    spread(s.qh, s.q1, Q_ONE)

    def own_scores(h):
        score = mm(block(s.kh, h), block(s.qh, h), 1, 1) * factor
        key_at = lax.broadcasted_iota(jnp.int32, (B, B), 0)
        query_at = lax.broadcasted_iota(jnp.int32, (B, B), 1)
        s.win[h, pl.ds(B, B)] = jnp.where(key_at <= query_at, score, -jnp.inf)
        s.gin[h] = (block(s.ch, h).astype(F32) * s.gain[:, lanes(h)]).T

    loop(0, X, own_scores)

    await_pieces(s.k1, K_ONE)
    choose(s.k2, s.k1, s.pairing)
    forward(s.k2, s.k3, K_TWO)
    relay_on(s.rk, s.pk, PASS_K, X - 1, over)
    await_pieces(s.v1, V_ONE)
    choose(s.v2, s.v1, s.pairing)
    forward(s.v2, s.v3, V_TWO)
    relay_on(s.rv, s.pv, PASS_V, X - 1, over)
    await_pieces(s.q1, Q_ONE)
    choose(s.q2, s.q1, s.inverse)
    forward(s.q2, s.q3, Q_TWO)

    await_bytes(s.pk, s.recv_sem.at[PASS_K])

    def prior_scores(h):
        score = mm(block(s.pk, h), block(s.qh, h), 1, 1) * factor
        s.win[h, pl.ds(0, B)] = jnp.where(ctx > 0, score, -jnp.inf)

    loop(0, X, prior_scores)
    await_bytes(s.pv, s.recv_sem.at[PASS_V])
    await_pieces(s.k3, K_TWO)

    def softmax(h):
        s.win[h, pl.ds(2 * B, B)] = mm(block(s.k3, h), block(s.qh, h), 1, 1) * factor
        score = s.win[h]
        highest = jnp.max(score, axis=0, keepdims=True)
        logsum = highest + jnp.log(jnp.sum(jnp.exp(score - highest), axis=0, keepdims=True))
        s.lse[h] = logsum
        w = jnp.exp(score - logsum)
        s.win[h] = w
        p = w.astype(BF16)
        s.probs[h] = p
        s.acc[h] = mm(block(s.pv, h), p[0:B], 0, 0) + mm(block(s.vh, h), p[B : 2 * B], 0, 0)

    loop(0, X, softmax)
    s.stats[hd] = jnp.zeros((8, B), F32)
    await_pieces(s.v3, V_TWO)

    def attend(h):
        o = s.acc[h] + mm(block(s.v3, h), s.probs[h, pl.ds(2 * B, B)], 0, 0)
        a = o.astype(BF16).astype(F32)
        s.att[h] = a
        s.stats[hd, 0:1] += jnp.sum(a * a, axis=0, keepdims=True)
        s.stats[hd, 1:2] += jnp.sum(s.gin[h] * a, axis=0, keepdims=True)

    loop(0, X, attend)
    each_head_peer(lambda g: remote(s.stats.at[hd], s.stats.at[hd], STATS, ctx, g).start())
    await_bytes(s.stats.at[pl.ds(0, G - 1)], s.recv_sem.at[STATS])
    total = jnp.sum(s.stats[...], axis=0)
    rms = lax.rsqrt(total[0:1] / features + EPSILON)
    slope = rms * rms * rms * (total[1:2] / features)

    def attn_grad(h):
        a = s.att[h]
        d = rms * s.gin[h] - a * slope
        low = d.astype(BF16)
        s.dat[h] = low
        s.d0[head_rows(h)] = d.T.astype(BF16).reshape(Z, ROWS, HD)
        delta = jnp.sum(low.astype(F32) * a, axis=0, keepdims=True)
        s.delta[h] = delta
        logsum = s.lse[h]
        for t in range(2):
            cut = slice(t * half, (t + 1) * half)
            s.e0[2 * h + t, 0:1] = logsum[:, cut]
            s.e0[2 * h + t, 1:2] = delta[:, cut]

    loop(0, X, attn_grad)

    rows = 2 * X
    gap = (N - 1) // (rows - 1)
    row = ctx // gap
    carries = ctx == row * gap
    for r in range(rows):

        @pl.when(ctx != r * gap)
        def _():
            remote(s.e0.at[r], s.e1.at[ctx], E_ONE, r * gap, hd).start()

        @pl.when(ctx == r * gap)
        def _():
            pltpu.make_async_copy(s.e0.at[r], s.e1.at[ctx], s.recv_sem.at[E_ONE]).start()

    s.d1[ctx] = s.d0[mine]
    spread(s.d0, s.d1, D_ONE)

    def score_grad(h, g, values):
        dp = mm(values, s.dat[h], 1, 0)
        d = (s.win[h, pl.ds(g * B, B)] * (dp - s.delta[h])).astype(BF16)
        s.dsc[h, pl.ds(g * B, B)] = d
        return d

    def prior_terms(h):
        d = score_grad(h, 0, block(s.pv, h))
        term = (mm(d, block(s.qh, h), 1, 0) * factor).astype(BF16)
        s.bk[head_rows(h)] = term.reshape(Z, ROWS, HD)
        term = mm(s.probs[h, pl.ds(0, B)], s.dat[h], 1, 1).astype(BF16)
        s.bv[head_rows(h)] = term.reshape(Z, ROWS, HD)

    loop(0, X, prior_terms)
    pass_on(s.bv, s.rbv, s.nv, BACK_V, 0, 1, before)
    pass_on(s.bk, s.rbk, s.nk, BACK_K, 0, 1, before)

    @pl.when(carries)
    def _():
        await_bytes(s.e1, s.recv_sem.at[E_ONE])
        choose(s.e2, s.e1, s.inverse)
        each_peer(lambda j: remote(s.e2.at[j], s.e3.at[row], E_TWO, j, hd).start())
        pltpu.make_async_copy(s.e2.at[ctx], s.e3.at[row], s.recv_sem.at[E_TWO]).start()

    def own_terms(h):
        d = score_grad(h, 1, block(s.vh, h))
        s.own_k[h] = mm(d, block(s.qh, h), 1, 0) * factor
        s.own_v[h] = mm(s.probs[h, pl.ds(B, B)], s.dat[h], 1, 1)

    loop(0, X, own_terms)

    await_pieces(s.d1, D_ONE)
    choose(s.d2, s.d1, s.inverse)
    each_peer(lambda j: remote(s.d2.at[j], s.d3.at[mine], D_TWO, j, hd, HEAD + my_head).start())
    pltpu.make_async_copy(s.d2.at[ctx], s.d3.at[mine], s.recv_sem.at[HEAD + my_head]).start()
    relay_on(s.rbv, s.nv, BACK_V, 0, under)
    relay_on(s.rbk, s.nk, BACK_K, 0, under)

    def query_terms(h):
        d = score_grad(h, 2, block(s.v3, h))
        gq = (
            mm(s.dsc[h, pl.ds(0, B)], block(s.pk, h), 0, 0)
            + mm(s.dsc[h, pl.ds(B, B)], block(s.kh, h), 0, 0)
            + mm(d, block(s.k3, h), 0, 0)
        )
        gq_out[:, lanes(h)] = (gq * factor).astype(BF16)
        mixed_out[:, lanes(h)] = ((s.att[h] * rms).T * s.gain[:, lanes(h)]).astype(BF16)

    loop(0, X, query_terms)

    await_pieces(s.q3, Q_TWO)
    await_bytes(s.e3, s.recv_sem.at[E_TWO])

    def incoming(h, n):
        return jnp.concatenate([s.e3[2 * h, n : n + 1], s.e3[2 * h + 1, n : n + 1]], axis=1)

    def incoming_probs(h):
        w = jnp.exp(mm(block(s.kh, h), block(s.q3, h), 1, 1) * factor - incoming(h, 0))
        s.win_in[h] = w
        s.probs_in[h] = w.astype(BF16)

    loop(0, X, incoming_probs)
    await_bytes(s.nv, s.recv_sem.at[BACK_V])
    await_bytes(s.nk, s.recv_sem.at[BACK_K])

    def add_next(h):
        s.own_v[h] += block(s.nv, h).astype(F32)
        s.own_k[h] += block(s.nk, h).astype(F32)

    loop(0, X, add_next)

    def partner_terms(h):
        await_bytes(s.d3.at[head_rows(h)], s.recv_sem.at[HEAD + h])
        d = block(s.d3, h)
        gv_out[:, lanes(h)] = (s.own_v[h] + mm(s.probs_in[h], d, 1, 0)).astype(BF16)
        dp = mm(block(s.vh, h), d, 1, 1)
        ds = (s.win_in[h] * (dp - incoming(h, 1))).astype(BF16)
        gk_out[:, lanes(h)] = (s.own_k[h] + mm(ds, block(s.q3, h), 1, 0) * factor).astype(BF16)

    loop(0, X, partner_terms)

    for n in (K_ONE, V_ONE, Q_ONE, D_ONE, K_TWO, V_TWO, Q_TWO, D_TWO):
        await_bytes(s.k1.at[pl.ds(0, N - 1)], s.send_sem.at[n])
    await_bytes(s.stats.at[pl.ds(0, G - 1)], s.send_sem.at[STATS])
    end_pass(s.kh, s.rk, PASS_K, X - 1)
    end_pass(s.vh, s.rv, PASS_V, X - 1)
    end_pass(s.bv, s.rbv, BACK_V, 0)
    end_pass(s.bk, s.rbk, BACK_K, 0)

    @pl.when(carries)
    def _():
        await_bytes(s.e0.at[pl.ds(0, rows - 1)], s.send_sem.at[E_ONE])
        await_bytes(s.e2.at[pl.ds(0, N - 1)], s.send_sem.at[E_TWO])

    @pl.when(jnp.logical_not(carries))
    def _():
        await_bytes(s.e0, s.send_sem.at[E_ONE])


def write_out(*refs):
    sem = refs[8]
    copies = [pltpu.make_async_copy(refs[n], refs[4 + n], sem.at[n]) for n in range(4)]
    for copy in copies:
        copy.start()
    for copy in copies:
        copy.wait()


def on_device(sizes, queries, key_rows, value_rows, cotangent, norm_gain, pairing):
    Z, X, G = sizes
    N, B, W = Z * X, Z * ROWS, X * HD
    tiles = (Z, ROWS, W)
    hbm = pl.BlockSpec(memory_space=pltpu.HBM)
    out = jax.ShapeDtypeStruct((B, W), BF16)
    held = pl.pallas_call(
        functools.partial(body, sizes),
        out_shape=(pltpu.VMEM((B, W), BF16),) * 4,
        in_specs=[hbm] * 6,
        out_specs=(pl.BlockSpec(memory_space=pltpu.VMEM),) * 4,
        scratch_shapes=list(scratch(sizes).values()),
        compiler_params=pltpu.CompilerParams(
            collective_id=0, has_side_effects=True, vmem_limit_bytes=56 << 20
        ),
    )(
        queries.reshape(tiles),
        key_rows.reshape(tiles),
        value_rows.reshape(tiles),
        cotangent.reshape(tiles),
        norm_gain.reshape(1, W),
        pairing.reshape(1, N),
    )
    return pl.pallas_call(
        write_out,
        out_shape=(out,) * 4,
        in_specs=[pl.BlockSpec(memory_space=pltpu.VMEM)] * 4,
        out_specs=(hbm,) * 4,
        scratch_shapes=[pltpu.SemaphoreType.DMA((4,))],
        compiler_params=pltpu.CompilerParams(vmem_limit_bytes=4 << 20),
    )(*held)


def solution(mesh):
    heads_here = 4
    sizes = (mesh.shape["ctx"] // heads_here, heads_here, mesh.shape["head"])
    spec = P("ctx", "head")
    return jax.shard_map(
        functools.partial(on_device, sizes),
        mesh=mesh,
        in_specs=(spec, spec, spec, spec, P("head"), P()),
        out_specs=(spec,) * 4,
        check_vma=False,
    )
```

```python
import functools
import math
import types

import jax
import jax.numpy as jnp
from jax import lax
from jax.experimental import pallas as pl
from jax.experimental.pallas import tpu as pltpu
from jax.sharding import PartitionSpec as P

HD = 128
ROWS = 16
EPSILON = 1e-05
MESH = pl.DeviceIdType.MESH
F32 = jnp.float32
BF16 = jnp.bfloat16

K_ONE, V_ONE, Q_ONE, D_ONE, K_TWO, V_TWO, Q_TWO, D_TWO = range(8)
PASS_K, PASS_V, RELAY_K, RELAY_V, BACK_V, BACK_K, RELAY_BV, RELAY_BK, STATS, E_ONE, E_TWO, HEAD = range(8, 20)


def mm(a, b, da, db):
    return lax.dot_general(a, b, (((da,), (db,)), ((), ())), preferred_element_type=F32)


def scratch(sizes):
    Z, X, G = sizes
    N, B, W = Z * X, Z * ROWS, X * HD
    pieces = pltpu.VMEM((N, ROWS, HD), BF16)
    part = pltpu.VMEM((Z, ROWS, HD), BF16)
    turned = pltpu.VMEM((X, HD, B), F32)
    upright = pltpu.VMEM((X, B, HD), F32)
    return dict(
        qh=pieces, kh=pieces, vh=pieces, ch=pieces,
        k1=pieces, v1=pieces, q1=pieces, d1=pieces,
        k2=pieces, v2=pieces, q2=pieces, d2=pieces,
        k3=pieces, v3=pieces, q3=pieces, d3=pieces,
        d0=pieces, pk=pieces, pv=pieces, bk=pieces, bv=pieces, nk=pieces, nv=pieces,
        rk=part, rv=part, rbk=part, rbv=part,
        win=pltpu.VMEM((X, 3 * B, B), F32),
        probs=pltpu.VMEM((X, 3 * B, B), BF16),
        dsc=pltpu.VMEM((X, 3 * B, B), BF16),
        win_in=pltpu.VMEM((X, B, B), F32),
        probs_in=pltpu.VMEM((X, B, B), BF16),
        acc=turned, gin=turned, att=turned,
        dat=pltpu.VMEM((X, HD, B), BF16),
        delta=pltpu.VMEM((X, 1, B), F32),
        lse=pltpu.VMEM((X, 1, B), F32),
        stats=pltpu.VMEM((G, 8, B), F32),
        e0=pltpu.VMEM((2 * X, 2, B // 2), F32),
        e1=pltpu.VMEM((N, 2, B // 2), F32),
        e2=pltpu.VMEM((N, 2, B // 2), F32),
        e3=pltpu.VMEM((2 * X, 2, B // 2), F32),
        own_k=upright, own_v=upright,
        gain=pltpu.VMEM((1, W), F32),
        pair_row=pltpu.VMEM((1, N), jnp.int32),
        inverse_row=pltpu.VMEM((1, N), jnp.int32),
        pairing=pltpu.SMEM((1, N), jnp.int32),
        inverse=pltpu.SMEM((1, N), jnp.int32),
        load_sem=pltpu.SemaphoreType.DMA((4 * X + 4,)),
        send_sem=pltpu.SemaphoreType.DMA((HEAD,)),
        recv_sem=pltpu.SemaphoreType.DMA((HEAD + X,)),
    )


def body(sizes, q_in, k_in, v_in, c_in, gain_in, pairing_in, mixed_out, gq_out, gk_out, gv_out, *refs):
    s = types.SimpleNamespace(**dict(zip(scratch(sizes), refs)))
    Z, X, G = sizes
    N = Z * X
    B = Z * ROWS
    half = B // 2
    factor = 1.0 / math.sqrt(HD)
    features = float(G * X * HD)
    ctx = lax.axis_index("ctx")
    hd = lax.axis_index("head")
    z = ctx // X
    x = lax.rem(ctx, X)

    def wrap(i, n):
        return jnp.where(i >= n, i - n, i)

    after = wrap(ctx + 1, N)
    before = wrap(ctx + N - 1, N)
    over = wrap(z + 1, Z) * X
    under = wrap(z + Z - 1, Z) * X + X - 1
    columns = [wrap(x + n, X) for n in range(X)]

    def via(h, zj):
        return zj * X + 2 * lax.rem(h, 2) + lax.rem(zj + h // 2, 2)

    my_head = 2 * lax.rem(x + z, 2) + x // 2
    mine = my_head * Z + z

    def lanes(h):
        return pl.ds(pl.multiple_of(h * HD, HD), HD)

    def head_rows(h):
        return pl.ds(pl.multiple_of(h * Z, Z), Z)

    def block(ref, h):
        return ref[head_rows(h)].reshape(B, HD)

    def remote(src, dst, n, j, g, m=None):
        return pltpu.make_async_remote_copy(
            src_ref=src,
            dst_ref=dst,
            send_sem=s.send_sem.at[n],
            recv_sem=s.recv_sem.at[n if m is None else m],
            device_id=(j, g),
            device_id_type=MESH,
        )

    def loop(lo, hi, f):
        def step(k, carry):
            f(k)
            return carry

        lax.fori_loop(lo, hi, step, 0)

    def each_peer(f):
        for n in range(1, X):
            f(z * X + columns[n])

        def along_z(k):
            zj = wrap(z + k, Z)
            for n in range(X):
                f(zj * X + columns[n])

        loop(1, Z, along_z)

    def each_head_peer(f):
        loop(1, G, lambda k: f(wrap(hd + k, G)))

    def await_bytes(ref, sem):
        pltpu.make_async_copy(ref, ref, sem).wait()

    barrier = pltpu.get_barrier_semaphore()
    each_peer(lambda j: pl.semaphore_signal(barrier, inc=1, device_id=(j, hd), device_id_type=MESH))
    each_head_peer(lambda g: pl.semaphore_signal(barrier, inc=1, device_id=(ctx, g), device_id_type=MESH))

    small = (
        pltpu.make_async_copy(pairing_in, s.pair_row, s.load_sem.at[4 * X + 1]),
        pltpu.make_async_copy(pairing_in, s.pairing, s.load_sem.at[4 * X + 2]),
        pltpu.make_async_copy(gain_in, s.gain, s.load_sem.at[4 * X]),
    )
    loads = []
    for n, (src, dst) in enumerate(((k_in, s.kh), (v_in, s.vh), (q_in, s.qh), (c_in, s.ch))):
        for h in range(X):
            loads.append(
                pltpu.make_async_copy(
                    src.at[:, :, pl.ds(h * HD, HD)], dst.at[pl.ds(h * Z, Z)], s.load_sem.at[n * X + h]
                )
            )
    for copy in loads[:X] + list(small) + loads[X:]:
        copy.start()
    for copy in small:
        copy.wait()
    down = lax.broadcasted_iota(jnp.int32, (N, N), 0)
    across = lax.broadcasted_iota(jnp.int32, (N, N), 1)
    partners = jnp.broadcast_to(s.pair_row[...], (N, N))
    partner_of = jnp.sum(jnp.where(down == across, partners, 0), axis=1, keepdims=True)
    s.inverse_row[...] = jnp.max(jnp.where(partner_of == across, down, 0), axis=0, keepdims=True)
    turn = pltpu.make_async_copy(s.inverse_row, s.inverse, s.load_sem.at[4 * X + 3])
    turn.start()
    for copy in loads:
        copy.wait()
    turn.wait()
    s.k1[ctx] = s.kh[mine]
    s.v1[ctx] = s.vh[mine]
    s.q1[ctx] = s.qh[mine]
    pl.semaphore_wait(barrier, N - 1 + G - 1)

    def pass_on(src, relay, dst, n, edge, step, target):
        @pl.when(x != edge)
        def _():
            remote(src, dst, n, target, hd).start()

        @pl.when(x == edge)
        def _():
            for h in range(1, X):
                by = edge + h * step
                part = pl.ds(by * Z, Z)
                remote(src.at[part], relay, n, z * X + by, hd, n + 2).start()
            part = pl.ds(edge * Z, Z)
            remote(src.at[part], dst.at[part], n, target, hd).start()

    def relay_on(relay, dst, n, edge, target):
        @pl.when(x != edge)
        def _():
            await_bytes(relay, s.recv_sem.at[n + 2])
            remote(relay, dst.at[head_rows(x)], n + 2, target, hd, n).start()

    def end_pass(src, relay, n, edge):
        await_bytes(src, s.send_sem.at[n])

        @pl.when(x != edge)
        def _():
            await_bytes(relay, s.send_sem.at[n + 2])

    def spread(src, dst, n):
        def of_head(h):
            def to(k):
                zj = wrap(z + k, Z)
                j = via(h, zj)

                @pl.when(j != ctx)
                def _():
                    remote(src.at[h * Z + zj], dst.at[ctx], n, j, hd).start()

            loop(0, Z, to)

        loop(0, X, of_head)

    def choose(dst, src, table):
        def f(j):
            dst[j] = src[table[0, j]]

        loop(0, N, f)

    def forward(src, dst, n):
        dst[mine] = src[ctx]
        each_peer(lambda j: remote(src.at[j], dst.at[mine], n, j, hd).start())

    def await_pieces(dst, n):
        await_bytes(dst.at[pl.ds(0, N - 1)], s.recv_sem.at[n])

    spread(s.kh, s.k1, K_ONE)
    pass_on(s.kh, s.rk, s.pk, PASS_K, X - 1, -1, after)
    spread(s.vh, s.v1, V_ONE)
    pass_on(s.vh, s.rv, s.pv, PASS_V, X - 1, -1, after)

    def own_scores(h):
        score = mm(block(s.kh, h), block(s.qh, h), 1, 1) * factor
        key_at = lax.broadcasted_iota(jnp.int32, (B, B), 0)
        query_at = lax.broadcasted_iota(jnp.int32, (B, B), 1)
        s.win[h, pl.ds(B, B)] = jnp.where(key_at <= query_at, score, -jnp.inf)
        s.gin[h] = (block(s.ch, h).astype(F32) * s.gain[:, lanes(h)]).T

    loop(0, X, own_scores)

    await_pieces(s.k1, K_ONE)
    choose(s.k2, s.k1, s.pairing)
    forward(s.k2, s.k3, K_TWO)
    relay_on(s.rk, s.pk, PASS_K, X - 1, over)
    await_pieces(s.v1, V_ONE)
    choose(s.v2, s.v1, s.pairing)
    forward(s.v2, s.v3, V_TWO)
    relay_on(s.rv, s.pv, PASS_V, X - 1, over)
    spread(s.qh, s.q1, Q_ONE)

    await_bytes(s.pk, s.recv_sem.at[PASS_K])

    def prior_scores(h):
        score = mm(block(s.pk, h), block(s.qh, h), 1, 1) * factor
        s.win[h, pl.ds(0, B)] = jnp.where(ctx > 0, score, -jnp.inf)

    loop(0, X, prior_scores)
    await_bytes(s.pv, s.recv_sem.at[PASS_V])
    await_pieces(s.k3, K_TWO)

    def softmax(h):
        s.win[h, pl.ds(2 * B, B)] = mm(block(s.k3, h), block(s.qh, h), 1, 1) * factor
        score = s.win[h]
        highest = jnp.max(score, axis=0, keepdims=True)
        logsum = highest + jnp.log(jnp.sum(jnp.exp(score - highest), axis=0, keepdims=True))
        s.lse[h] = logsum
        w = jnp.exp(score - logsum)
        s.win[h] = w
        p = w.astype(BF16)
        s.probs[h] = p
        s.acc[h] = mm(block(s.pv, h), p[0:B], 0, 0) + mm(block(s.vh, h), p[B : 2 * B], 0, 0)

    loop(0, X, softmax)
    s.stats[hd] = jnp.zeros((8, B), F32)
    await_pieces(s.v3, V_TWO)

    def attend(h):
        o = s.acc[h] + mm(block(s.v3, h), s.probs[h, pl.ds(2 * B, B)], 0, 0)
        a = o.astype(BF16).astype(F32)
        s.att[h] = a
        s.stats[hd, 0:1] += jnp.sum(a * a, axis=0, keepdims=True)
        s.stats[hd, 1:2] += jnp.sum(s.gin[h] * a, axis=0, keepdims=True)

    loop(0, X, attend)
    each_head_peer(lambda g: remote(s.stats.at[hd], s.stats.at[hd], STATS, ctx, g).start())
    await_bytes(s.stats.at[pl.ds(0, G - 1)], s.recv_sem.at[STATS])
    total = jnp.sum(s.stats[...], axis=0)
    rms = lax.rsqrt(total[0:1] / features + EPSILON)
    slope = rms * rms * rms * (total[1:2] / features)

    def attn_grad(h):
        a = s.att[h]
        d = rms * s.gin[h] - a * slope
        low = d.astype(BF16)
        s.dat[h] = low
        s.d0[head_rows(h)] = d.T.astype(BF16).reshape(Z, ROWS, HD)
        delta = jnp.sum(low.astype(F32) * a, axis=0, keepdims=True)
        s.delta[h] = delta
        logsum = s.lse[h]
        for t in range(2):
            cut = slice(t * half, (t + 1) * half)
            s.e0[2 * h + t, 0:1] = logsum[:, cut]
            s.e0[2 * h + t, 1:2] = delta[:, cut]

    loop(0, X, attn_grad)

    rows = 2 * X
    gap = (N - 1) // (rows - 1)
    row = ctx // gap
    carries = ctx == row * gap
    for r in range(rows):

        @pl.when(ctx != r * gap)
        def _():
            remote(s.e0.at[r], s.e1.at[ctx], E_ONE, r * gap, hd).start()

        @pl.when(ctx == r * gap)
        def _():
            pltpu.make_async_copy(s.e0.at[r], s.e1.at[ctx], s.recv_sem.at[E_ONE]).start()

    s.d1[ctx] = s.d0[mine]
    spread(s.d0, s.d1, D_ONE)

    await_pieces(s.q1, Q_ONE)
    choose(s.q2, s.q1, s.inverse)
    forward(s.q2, s.q3, Q_TWO)

    def score_grad(h, g, values):
        dp = mm(values, s.dat[h], 1, 0)
        d = (s.win[h, pl.ds(g * B, B)] * (dp - s.delta[h])).astype(BF16)
        s.dsc[h, pl.ds(g * B, B)] = d
        return d

    def prior_terms(h):
        d = score_grad(h, 0, block(s.pv, h))
        term = (mm(d, block(s.qh, h), 1, 0) * factor).astype(BF16)
        s.bk[head_rows(h)] = term.reshape(Z, ROWS, HD)
        term = mm(s.probs[h, pl.ds(0, B)], s.dat[h], 1, 1).astype(BF16)
        s.bv[head_rows(h)] = term.reshape(Z, ROWS, HD)

    loop(0, X, prior_terms)
    pass_on(s.bv, s.rbv, s.nv, BACK_V, 0, 1, before)
    pass_on(s.bk, s.rbk, s.nk, BACK_K, 0, 1, before)

    @pl.when(carries)
    def _():
        await_bytes(s.e1, s.recv_sem.at[E_ONE])
        choose(s.e2, s.e1, s.inverse)
        each_peer(lambda j: remote(s.e2.at[j], s.e3.at[row], E_TWO, j, hd).start())
        pltpu.make_async_copy(s.e2.at[ctx], s.e3.at[row], s.recv_sem.at[E_TWO]).start()

    def own_terms(h):
        d = score_grad(h, 1, block(s.vh, h))
        s.own_k[h] = mm(d, block(s.qh, h), 1, 0) * factor
        s.own_v[h] = mm(s.probs[h, pl.ds(B, B)], s.dat[h], 1, 1)

    loop(0, X, own_terms)

    await_pieces(s.d1, D_ONE)
    choose(s.d2, s.d1, s.inverse)
    each_peer(lambda j: remote(s.d2.at[j], s.d3.at[mine], D_TWO, j, hd, HEAD + my_head).start())
    pltpu.make_async_copy(s.d2.at[ctx], s.d3.at[mine], s.recv_sem.at[HEAD + my_head]).start()
    relay_on(s.rbv, s.nv, BACK_V, 0, under)
    relay_on(s.rbk, s.nk, BACK_K, 0, under)

    def query_terms(h):
        d = score_grad(h, 2, block(s.v3, h))
        gq = (
            mm(s.dsc[h, pl.ds(0, B)], block(s.pk, h), 0, 0)
            + mm(s.dsc[h, pl.ds(B, B)], block(s.kh, h), 0, 0)
            + mm(d, block(s.k3, h), 0, 0)
        )
        gq_out[:, lanes(h)] = (gq * factor).astype(BF16)
        mixed_out[:, lanes(h)] = ((s.att[h] * rms).T * s.gain[:, lanes(h)]).astype(BF16)

    loop(0, X, query_terms)

    await_pieces(s.q3, Q_TWO)
    await_bytes(s.e3, s.recv_sem.at[E_TWO])

    def incoming(h, n):
        return jnp.concatenate([s.e3[2 * h, n : n + 1], s.e3[2 * h + 1, n : n + 1]], axis=1)

    def incoming_probs(h):
        w = jnp.exp(mm(block(s.kh, h), block(s.q3, h), 1, 1) * factor - incoming(h, 0))
        s.win_in[h] = w
        s.probs_in[h] = w.astype(BF16)

    loop(0, X, incoming_probs)
    await_bytes(s.nv, s.recv_sem.at[BACK_V])
    await_bytes(s.nk, s.recv_sem.at[BACK_K])

    def add_next(h):
        s.own_v[h] += block(s.nv, h).astype(F32)
        s.own_k[h] += block(s.nk, h).astype(F32)

    loop(0, X, add_next)

    def partner_terms(h):
        await_bytes(s.d3.at[head_rows(h)], s.recv_sem.at[HEAD + h])
        d = block(s.d3, h)
        gv_out[:, lanes(h)] = (s.own_v[h] + mm(s.probs_in[h], d, 1, 0)).astype(BF16)
        dp = mm(block(s.vh, h), d, 1, 1)
        ds = (s.win_in[h] * (dp - incoming(h, 1))).astype(BF16)
        gk_out[:, lanes(h)] = (s.own_k[h] + mm(ds, block(s.q3, h), 1, 0) * factor).astype(BF16)

    loop(0, X, partner_terms)

    for n in (K_ONE, V_ONE, Q_ONE, D_ONE, K_TWO, V_TWO, Q_TWO, D_TWO):
        await_bytes(s.k1.at[pl.ds(0, N - 1)], s.send_sem.at[n])
    await_bytes(s.stats.at[pl.ds(0, G - 1)], s.send_sem.at[STATS])
    end_pass(s.kh, s.rk, PASS_K, X - 1)
    end_pass(s.vh, s.rv, PASS_V, X - 1)
    end_pass(s.bv, s.rbv, BACK_V, 0)
    end_pass(s.bk, s.rbk, BACK_K, 0)

    @pl.when(carries)
    def _():
        await_bytes(s.e0.at[pl.ds(0, rows - 1)], s.send_sem.at[E_ONE])
        await_bytes(s.e2.at[pl.ds(0, N - 1)], s.send_sem.at[E_TWO])

    @pl.when(jnp.logical_not(carries))
    def _():
        await_bytes(s.e0, s.send_sem.at[E_ONE])


def write_out(*refs):
    sem = refs[8]
    copies = [pltpu.make_async_copy(refs[n], refs[4 + n], sem.at[n]) for n in range(4)]
    for copy in copies:
        copy.start()
    for copy in copies:
        copy.wait()


def on_device(sizes, queries, key_rows, value_rows, cotangent, norm_gain, pairing):
    Z, X, G = sizes
    N, B, W = Z * X, Z * ROWS, X * HD
    tiles = (Z, ROWS, W)
    hbm = pl.BlockSpec(memory_space=pltpu.HBM)
    out = jax.ShapeDtypeStruct((B, W), BF16)
    held = pl.pallas_call(
        functools.partial(body, sizes),
        out_shape=(pltpu.VMEM((B, W), BF16),) * 4,
        in_specs=[hbm] * 6,
        out_specs=(pl.BlockSpec(memory_space=pltpu.VMEM),) * 4,
        scratch_shapes=list(scratch(sizes).values()),
        compiler_params=pltpu.CompilerParams(
            collective_id=0, has_side_effects=True, vmem_limit_bytes=56 << 20
        ),
    )(
        queries.reshape(tiles),
        key_rows.reshape(tiles),
        value_rows.reshape(tiles),
        cotangent.reshape(tiles),
        norm_gain.reshape(1, W),
        pairing.reshape(1, N),
    )
    return pl.pallas_call(
        write_out,
        out_shape=(out,) * 4,
        in_specs=[pl.BlockSpec(memory_space=pltpu.VMEM)] * 4,
        out_specs=(hbm,) * 4,
        scratch_shapes=[pltpu.SemaphoreType.DMA((4,))],
        compiler_params=pltpu.CompilerParams(vmem_limit_bytes=4 << 20),
    )(*held)


def solution(mesh):
    heads_here = 4
    sizes = (mesh.shape["ctx"] // heads_here, heads_here, mesh.shape["head"])
    spec = P("ctx", "head")
    return jax.shard_map(
        functools.partial(on_device, sizes),
        mesh=mesh,
        in_specs=(spec, spec, spec, spec, P("head"), P()),
        out_specs=(spec,) * 4,
        check_vma=False,
    )
```

```python
import functools
import math
import types

import jax
import jax.numpy as jnp
from jax import lax
from jax.experimental import pallas as pl
from jax.experimental.pallas import tpu as pltpu
from jax.sharding import PartitionSpec as P

HD = 128
ROWS = 16
EPSILON = 1e-05
MESH = pl.DeviceIdType.MESH
F32 = jnp.float32
BF16 = jnp.bfloat16

K_ONE, V_ONE, Q_ONE, D_ONE, K_TWO, V_TWO, Q_TWO, D_TWO = range(8)
PASS_K, PASS_V, RELAY_K, RELAY_V, BACK_V, BACK_K, RELAY_BV, RELAY_BK, STATS, E_ONE, E_TWO, HEAD = range(8, 20)


def mm(a, b, da, db):
    return lax.dot_general(a, b, (((da,), (db,)), ((), ())), preferred_element_type=F32)


def scratch(sizes):
    Z, X, G = sizes
    N, B, W = Z * X, Z * ROWS, X * HD
    pieces = pltpu.VMEM((N, ROWS, HD), BF16)
    part = pltpu.VMEM((Z, ROWS, HD), BF16)
    turned = pltpu.VMEM((X, HD, B), F32)
    upright = pltpu.VMEM((X, B, HD), F32)
    return dict(
        qh=pieces, kh=pieces, vh=pieces, ch=pieces,
        k1=pieces, v1=pieces, q1=pieces, d1=pieces,
        k2=pieces, v2=pieces, q2=pieces, d2=pieces,
        k3=pieces, v3=pieces, q3=pieces, d3=pieces,
        d0=pieces, pk=pieces, pv=pieces, bk=pieces, bv=pieces, nk=pieces, nv=pieces,
        rk=part, rv=part, rbk=part, rbv=part,
        win=pltpu.VMEM((X, 3 * B, B), F32),
        probs=pltpu.VMEM((X, 3 * B, B), BF16),
        dsc=pltpu.VMEM((X, 3 * B, B), BF16),
        win_in=pltpu.VMEM((X, B, B), F32),
        probs_in=pltpu.VMEM((X, B, B), BF16),
        acc=turned, gin=turned, att=turned,
        dat=pltpu.VMEM((X, HD, B), BF16),
        delta=pltpu.VMEM((X, 1, B), F32),
        lse=pltpu.VMEM((X, 1, B), F32),
        stats=pltpu.VMEM((G, 2, B), F32),
        e0=pltpu.VMEM((2 * X, 2, B // 2), F32),
        e1=pltpu.VMEM((N, 2, B // 2), F32),
        e2=pltpu.VMEM((N, 2, B // 2), F32),
        e3=pltpu.VMEM((2 * X, 2, B // 2), F32),
        own_k=upright, own_v=upright,
        gain=pltpu.VMEM((1, W), F32),
        pair_row=pltpu.VMEM((1, N), jnp.int32),
        inverse_row=pltpu.VMEM((1, N), jnp.int32),
        pairing=pltpu.SMEM((1, N), jnp.int32),
        inverse=pltpu.SMEM((1, N), jnp.int32),
        load_sem=pltpu.SemaphoreType.DMA((4 * X + 4,)),
        send_sem=pltpu.SemaphoreType.DMA((HEAD,)),
        recv_sem=pltpu.SemaphoreType.DMA((HEAD + 2 * X,)),
    )


def body(sizes, q_in, k_in, v_in, c_in, gain_in, pairing_in, mixed_out, gq_out, gk_out, gv_out, *refs):
    s = types.SimpleNamespace(**dict(zip(scratch(sizes), refs)))
    Z, X, G = sizes
    N = Z * X
    B = Z * ROWS
    half = B // 2
    factor = 1.0 / math.sqrt(HD)
    features = float(G * X * HD)
    ctx = lax.axis_index("ctx")
    hd = lax.axis_index("head")
    z = ctx // X
    x = lax.rem(ctx, X)

    def wrap(i, n):
        return jnp.where(i >= n, i - n, i)

    after = wrap(ctx + 1, N)
    before = wrap(ctx + N - 1, N)
    over = wrap(z + 1, Z) * X
    under = wrap(z + Z - 1, Z) * X + X - 1
    columns = [wrap(x + n, X) for n in range(X)]

    def via(h, zj):
        return zj * X + 2 * lax.rem(h, 2) + lax.rem(zj + h // 2, 2)

    my_head = 2 * lax.rem(x + z, 2) + x // 2
    mine = my_head * Z + z

    def lanes(h):
        return pl.ds(pl.multiple_of(h * HD, HD), HD)

    def head_rows(h):
        return pl.ds(pl.multiple_of(h * Z, Z), Z)

    def block(ref, h):
        return ref[head_rows(h)].reshape(B, HD)

    def remote(src, dst, n, j, g, m=None):
        return pltpu.make_async_remote_copy(
            src_ref=src,
            dst_ref=dst,
            send_sem=s.send_sem.at[n],
            recv_sem=s.recv_sem.at[n if m is None else m],
            device_id=(j, g),
            device_id_type=MESH,
        )

    def loop(lo, hi, f):
        def step(k, carry):
            f(k)
            return carry

        lax.fori_loop(lo, hi, step, 0)

    def each_peer(f):
        for n in range(1, X):
            f(z * X + columns[n])

        def along_z(k):
            zj = wrap(z + k, Z)
            for n in range(X):
                f(zj * X + columns[n])

        loop(1, Z, along_z)

    def each_head_peer(f):
        loop(1, G, lambda k: f(wrap(hd + k, G)))

    def await_bytes(ref, sem):
        pltpu.make_async_copy(ref, ref, sem).wait()

    barrier = pltpu.get_barrier_semaphore()
    each_peer(lambda j: pl.semaphore_signal(barrier, inc=1, device_id=(j, hd), device_id_type=MESH))
    each_head_peer(lambda g: pl.semaphore_signal(barrier, inc=1, device_id=(ctx, g), device_id_type=MESH))

    small = (
        pltpu.make_async_copy(pairing_in, s.pair_row, s.load_sem.at[4 * X + 1]),
        pltpu.make_async_copy(pairing_in, s.pairing, s.load_sem.at[4 * X + 2]),
        pltpu.make_async_copy(gain_in, s.gain, s.load_sem.at[4 * X]),
    )
    loads = []
    for n, (src, dst) in enumerate(((k_in, s.kh), (v_in, s.vh), (q_in, s.qh), (c_in, s.ch))):
        for h in range(X):
            loads.append(
                pltpu.make_async_copy(
                    src.at[:, :, pl.ds(h * HD, HD)], dst.at[pl.ds(h * Z, Z)], s.load_sem.at[n * X + h]
                )
            )
    for copy in loads[:X] + list(small) + loads[X:]:
        copy.start()
    for copy in small:
        copy.wait()
    down = lax.broadcasted_iota(jnp.int32, (N, N), 0)
    across = lax.broadcasted_iota(jnp.int32, (N, N), 1)
    partners = jnp.broadcast_to(s.pair_row[...], (N, N))
    partner_of = jnp.sum(jnp.where(down == across, partners, 0), axis=1, keepdims=True)
    s.inverse_row[...] = jnp.max(jnp.where(partner_of == across, down, 0), axis=0, keepdims=True)
    turn = pltpu.make_async_copy(s.inverse_row, s.inverse, s.load_sem.at[4 * X + 3])
    turn.start()
    for copy in loads:
        copy.wait()
    turn.wait()
    s.k1[ctx] = s.kh[mine]
    s.v1[ctx] = s.vh[mine]
    s.q1[ctx] = s.qh[mine]
    pl.semaphore_wait(barrier, N - 1 + G - 1)

    def pass_on(src, relay, dst, n, edge, step, target):
        @pl.when(x != edge)
        def _():
            remote(src, dst, n, target, hd).start()

        @pl.when(x == edge)
        def _():
            for h in range(1, X):
                by = edge + h * step
                part = pl.ds(by * Z, Z)
                remote(src.at[part], relay, n, z * X + by, hd, n + 2).start()
            part = pl.ds(edge * Z, Z)
            remote(src.at[part], dst.at[part], n, target, hd).start()

    def relay_on(relay, dst, n, edge, target):
        @pl.when(x != edge)
        def _():
            await_bytes(relay, s.recv_sem.at[n + 2])
            remote(relay, dst.at[head_rows(x)], n + 2, target, hd, n).start()

    def end_pass(src, relay, n, edge):
        await_bytes(src, s.send_sem.at[n])

        @pl.when(x != edge)
        def _():
            await_bytes(relay, s.send_sem.at[n + 2])

    def spread_head(src, dst, n, h):
        def to(k):
            zj = wrap(z + k, Z)
            j = via(h, zj)

            @pl.when(j != ctx)
            def _():
                remote(src.at[h * Z + zj], dst.at[ctx], n, j, hd).start()

        loop(0, Z, to)

    def spread(src, dst, n):
        loop(0, X, lambda h: spread_head(src, dst, n, h))

    def choose(dst, src, table):
        def f(j):
            dst[j] = src[table[0, j]]

        loop(0, N, f)

    def forward(src, dst, n):
        dst[mine] = src[ctx]
        each_peer(lambda j: remote(src.at[j], dst.at[mine], n, j, hd).start())

    def await_pieces(dst, n):
        await_bytes(dst.at[pl.ds(0, N - 1)], s.recv_sem.at[n])

    spread(s.kh, s.k1, K_ONE)
    pass_on(s.kh, s.rk, s.pk, PASS_K, X - 1, -1, after)
    spread(s.vh, s.v1, V_ONE)
    pass_on(s.vh, s.rv, s.pv, PASS_V, X - 1, -1, after)

    def own_scores(h):
        score = mm(block(s.kh, h), block(s.qh, h), 1, 1) * factor
        key_at = lax.broadcasted_iota(jnp.int32, (B, B), 0)
        query_at = lax.broadcasted_iota(jnp.int32, (B, B), 1)
        s.win[h, pl.ds(B, B)] = jnp.where(key_at <= query_at, score, -jnp.inf)
        s.gin[h] = (block(s.ch, h).astype(F32) * s.gain[:, lanes(h)]).T

    loop(0, X, own_scores)

    await_pieces(s.k1, K_ONE)
    choose(s.k2, s.k1, s.pairing)
    forward(s.k2, s.k3, K_TWO)
    relay_on(s.rk, s.pk, PASS_K, X - 1, over)
    await_pieces(s.v1, V_ONE)
    choose(s.v2, s.v1, s.pairing)
    each_peer(lambda j: remote(s.v2.at[j], s.v3.at[mine], V_TWO, j, hd, HEAD + X + my_head).start())
    pltpu.make_async_copy(s.v2.at[ctx], s.v3.at[mine], s.recv_sem.at[HEAD + X + my_head]).start()
    relay_on(s.rv, s.pv, PASS_V, X - 1, over)
    spread(s.qh, s.q1, Q_ONE)

    await_bytes(s.pk, s.recv_sem.at[PASS_K])

    def prior_scores(h):
        score = mm(block(s.pk, h), block(s.qh, h), 1, 1) * factor
        s.win[h, pl.ds(0, B)] = jnp.where(ctx > 0, score, -jnp.inf)

    loop(0, X, prior_scores)
    await_bytes(s.pv, s.recv_sem.at[PASS_V])
    await_pieces(s.k3, K_TWO)

    def softmax(h):
        s.win[h, pl.ds(2 * B, B)] = mm(block(s.k3, h), block(s.qh, h), 1, 1) * factor
        score = s.win[h]
        highest = jnp.max(score, axis=0, keepdims=True)
        logsum = highest + jnp.log(jnp.sum(jnp.exp(score - highest), axis=0, keepdims=True))
        s.lse[h] = logsum
        w = jnp.exp(score - logsum)
        s.win[h] = w
        p = w.astype(BF16)
        s.probs[h] = p
        s.acc[h] = mm(block(s.pv, h), p[0:B], 0, 0) + mm(block(s.vh, h), p[B : 2 * B], 0, 0)

    loop(0, X, softmax)
    s.stats[hd] = jnp.zeros((2, B), F32)

    def attend(h):
        await_bytes(s.v3.at[head_rows(h)], s.recv_sem.at[HEAD + X + h])
        o = s.acc[h] + mm(block(s.v3, h), s.probs[h, pl.ds(2 * B, B)], 0, 0)
        a = o.astype(BF16).astype(F32)
        s.att[h] = a
        s.stats[hd, 0:1] += jnp.sum(a * a, axis=0, keepdims=True)
        s.stats[hd, 1:2] += jnp.sum(s.gin[h] * a, axis=0, keepdims=True)

    loop(0, X, attend)
    each_head_peer(lambda g: remote(s.stats.at[hd], s.stats.at[hd], STATS, ctx, g).start())
    await_bytes(s.stats.at[pl.ds(0, G - 1)], s.recv_sem.at[STATS])
    total = jnp.sum(s.stats[...], axis=0)
    rms = lax.rsqrt(total[0:1] / features + EPSILON)
    slope = rms * rms * rms * (total[1:2] / features)

    def attn_grad(h):
        a = s.att[h]
        d = rms * s.gin[h] - a * slope
        low = d.astype(BF16)
        s.dat[h] = low
        s.d0[head_rows(h)] = d.T.astype(BF16).reshape(Z, ROWS, HD)
        spread_head(s.d0, s.d1, D_ONE, h)
        delta = jnp.sum(low.astype(F32) * a, axis=0, keepdims=True)
        s.delta[h] = delta
        logsum = s.lse[h]
        for t in range(2):
            cut = slice(t * half, (t + 1) * half)
            s.e0[2 * h + t, 0:1] = logsum[:, cut]
            s.e0[2 * h + t, 1:2] = delta[:, cut]

    loop(0, X, attn_grad)

    rows = 2 * X
    gap = (N - 1) // (rows - 1)
    row = ctx // gap
    carries = ctx == row * gap
    for r in range(rows):

        @pl.when(ctx != r * gap)
        def _():
            remote(s.e0.at[r], s.e1.at[ctx], E_ONE, r * gap, hd).start()

        @pl.when(ctx == r * gap)
        def _():
            pltpu.make_async_copy(s.e0.at[r], s.e1.at[ctx], s.recv_sem.at[E_ONE]).start()

    s.d1[ctx] = s.d0[mine]

    await_pieces(s.q1, Q_ONE)
    choose(s.q2, s.q1, s.inverse)
    forward(s.q2, s.q3, Q_TWO)

    def score_grad(h, g, values):
        dp = mm(values, s.dat[h], 1, 0)
        d = (s.win[h, pl.ds(g * B, B)] * (dp - s.delta[h])).astype(BF16)
        s.dsc[h, pl.ds(g * B, B)] = d
        return d

    def prior_terms(h):
        d = score_grad(h, 0, block(s.pv, h))
        term = (mm(d, block(s.qh, h), 1, 0) * factor).astype(BF16)
        s.bk[head_rows(h)] = term.reshape(Z, ROWS, HD)
        term = mm(s.probs[h, pl.ds(0, B)], s.dat[h], 1, 1).astype(BF16)
        s.bv[head_rows(h)] = term.reshape(Z, ROWS, HD)

    loop(0, X, prior_terms)
    pass_on(s.bv, s.rbv, s.nv, BACK_V, 0, 1, before)
    pass_on(s.bk, s.rbk, s.nk, BACK_K, 0, 1, before)

    @pl.when(carries)
    def _():
        await_bytes(s.e1, s.recv_sem.at[E_ONE])
        choose(s.e2, s.e1, s.inverse)
        each_peer(lambda j: remote(s.e2.at[j], s.e3.at[row], E_TWO, j, hd).start())
        pltpu.make_async_copy(s.e2.at[ctx], s.e3.at[row], s.recv_sem.at[E_TWO]).start()

    def own_terms(h):
        d = score_grad(h, 1, block(s.vh, h))
        s.own_k[h] = mm(d, block(s.qh, h), 1, 0) * factor
        s.own_v[h] = mm(s.probs[h, pl.ds(B, B)], s.dat[h], 1, 1)

    loop(0, X, own_terms)

    await_pieces(s.d1, D_ONE)
    choose(s.d2, s.d1, s.inverse)
    each_peer(lambda j: remote(s.d2.at[j], s.d3.at[mine], D_TWO, j, hd, HEAD + my_head).start())
    pltpu.make_async_copy(s.d2.at[ctx], s.d3.at[mine], s.recv_sem.at[HEAD + my_head]).start()
    relay_on(s.rbv, s.nv, BACK_V, 0, under)
    relay_on(s.rbk, s.nk, BACK_K, 0, under)

    def query_terms(h):
        d = score_grad(h, 2, block(s.v3, h))
        gq = (
            mm(s.dsc[h, pl.ds(0, B)], block(s.pk, h), 0, 0)
            + mm(s.dsc[h, pl.ds(B, B)], block(s.kh, h), 0, 0)
            + mm(d, block(s.k3, h), 0, 0)
        )
        gq_out[:, lanes(h)] = (gq * factor).astype(BF16)
        mixed_out[:, lanes(h)] = ((s.att[h] * rms).T * s.gain[:, lanes(h)]).astype(BF16)

    loop(0, X, query_terms)

    await_pieces(s.q3, Q_TWO)
    await_bytes(s.e3, s.recv_sem.at[E_TWO])

    def incoming(h, n):
        return jnp.concatenate([s.e3[2 * h, n : n + 1], s.e3[2 * h + 1, n : n + 1]], axis=1)

    def incoming_probs(h):
        w = jnp.exp(mm(block(s.kh, h), block(s.q3, h), 1, 1) * factor - incoming(h, 0))
        s.win_in[h] = w
        s.probs_in[h] = w.astype(BF16)

    loop(0, X, incoming_probs)
    await_bytes(s.nv, s.recv_sem.at[BACK_V])
    await_bytes(s.nk, s.recv_sem.at[BACK_K])

    def add_next(h):
        s.own_v[h] += block(s.nv, h).astype(F32)
        s.own_k[h] += block(s.nk, h).astype(F32)

    loop(0, X, add_next)

    def partner_terms(h):
        await_bytes(s.d3.at[head_rows(h)], s.recv_sem.at[HEAD + h])
        d = block(s.d3, h)
        gv_out[:, lanes(h)] = (s.own_v[h] + mm(s.probs_in[h], d, 1, 0)).astype(BF16)
        dp = mm(block(s.vh, h), d, 1, 1)
        ds = (s.win_in[h] * (dp - incoming(h, 1))).astype(BF16)
        gk_out[:, lanes(h)] = (s.own_k[h] + mm(ds, block(s.q3, h), 1, 0) * factor).astype(BF16)

    loop(0, X, partner_terms)

    for n in (K_ONE, V_ONE, Q_ONE, D_ONE, K_TWO, V_TWO, Q_TWO, D_TWO):
        await_bytes(s.k1.at[pl.ds(0, N - 1)], s.send_sem.at[n])
    await_bytes(s.stats.at[pl.ds(0, G - 1)], s.send_sem.at[STATS])
    end_pass(s.kh, s.rk, PASS_K, X - 1)
    end_pass(s.vh, s.rv, PASS_V, X - 1)
    end_pass(s.bv, s.rbv, BACK_V, 0)
    end_pass(s.bk, s.rbk, BACK_K, 0)

    @pl.when(carries)
    def _():
        await_bytes(s.e0.at[pl.ds(0, rows - 1)], s.send_sem.at[E_ONE])
        await_bytes(s.e2.at[pl.ds(0, N - 1)], s.send_sem.at[E_TWO])

    @pl.when(jnp.logical_not(carries))
    def _():
        await_bytes(s.e0, s.send_sem.at[E_ONE])


def write_out(*refs):
    sem = refs[8]
    copies = [pltpu.make_async_copy(refs[n], refs[4 + n], sem.at[n]) for n in range(4)]
    for copy in copies:
        copy.start()
    for copy in copies:
        copy.wait()


def on_device(sizes, queries, key_rows, value_rows, cotangent, norm_gain, pairing):
    Z, X, G = sizes
    N, B, W = Z * X, Z * ROWS, X * HD
    tiles = (Z, ROWS, W)
    hbm = pl.BlockSpec(memory_space=pltpu.HBM)
    out = jax.ShapeDtypeStruct((B, W), BF16)
    held = pl.pallas_call(
        functools.partial(body, sizes),
        out_shape=(pltpu.VMEM((B, W), BF16),) * 4,
        in_specs=[hbm] * 6,
        out_specs=(pl.BlockSpec(memory_space=pltpu.VMEM),) * 4,
        scratch_shapes=list(scratch(sizes).values()),
        compiler_params=pltpu.CompilerParams(
            collective_id=0, has_side_effects=True, vmem_limit_bytes=56 << 20
        ),
    )(
        queries.reshape(tiles),
        key_rows.reshape(tiles),
        value_rows.reshape(tiles),
        cotangent.reshape(tiles),
        norm_gain.reshape(1, W),
        pairing.reshape(1, N),
    )
    return pl.pallas_call(
        write_out,
        out_shape=(out,) * 4,
        in_specs=[pl.BlockSpec(memory_space=pltpu.VMEM)] * 4,
        out_specs=(hbm,) * 4,
        scratch_shapes=[pltpu.SemaphoreType.DMA((4,))],
        compiler_params=pltpu.CompilerParams(vmem_limit_bytes=4 << 20),
    )(*held)


def solution(mesh):
    heads_here = 4
    sizes = (mesh.shape["ctx"] // heads_here, heads_here, mesh.shape["head"])
    spec = P("ctx", "head")
    return jax.shard_map(
        functools.partial(on_device, sizes),
        mesh=mesh,
        in_specs=(spec, spec, spec, spec, P("head"), P()),
        out_specs=(spec,) * 4,
        check_vma=False,
    )
```

```python
import functools
import math
import types

import jax
import jax.numpy as jnp
from jax import lax
from jax.experimental import pallas as pl
from jax.experimental.pallas import tpu as pltpu
from jax.sharding import PartitionSpec as P

HD = 128
ROWS = 16
EPSILON = 1e-05
MESH = pl.DeviceIdType.MESH
F32 = jnp.float32
BF16 = jnp.bfloat16

K_ONE, V_ONE, Q_ONE, D_ONE, K_TWO, V_TWO, Q_TWO, D_TWO = range(8)
PASS_K, PASS_V, RELAY_K, RELAY_V, BACK_V, BACK_K, RELAY_BV, RELAY_BK, STATS, E_ONE, E_TWO, HEAD = range(8, 20)


def mm(a, b, da, db):
    return lax.dot_general(a, b, (((da,), (db,)), ((), ())), preferred_element_type=F32)


def scratch(sizes):
    Z, X, G = sizes
    N, B, W = Z * X, Z * ROWS, X * HD
    pieces = pltpu.VMEM((N, ROWS, HD), BF16)
    part = pltpu.VMEM((Z, ROWS, HD), BF16)
    turned = pltpu.VMEM((X, HD, B), F32)
    upright = pltpu.VMEM((X, B, HD), F32)
    return dict(
        qh=pieces, kh=pieces, vh=pieces, ch=pieces,
        k1=pieces, v1=pieces, q1=pieces, d1=pieces,
        k2=pieces, v2=pieces, q2=pieces, d2=pieces,
        k3=pieces, v3=pieces, q3=pieces, d3=pieces,
        d0=pieces, pk=pieces, pv=pieces, bk=pieces, bv=pieces, nk=pieces, nv=pieces,
        rk=part, rv=part, rbk=part, rbv=part,
        win=pltpu.VMEM((X, 3 * B, B), F32),
        probs=pltpu.VMEM((X, 3 * B, B), BF16),
        dsc=pltpu.VMEM((X, 3 * B, B), BF16),
        win_in=pltpu.VMEM((X, B, B), F32),
        probs_in=pltpu.VMEM((X, B, B), BF16),
        acc=turned, gin=turned, att=turned,
        dat=pltpu.VMEM((X, HD, B), BF16),
        delta=pltpu.VMEM((X, 1, B), F32),
        lse=pltpu.VMEM((X, 1, B), F32),
        stats=pltpu.VMEM((G, 2, B), F32),
        e0=pltpu.VMEM((2 * X, 2, B // 2), F32),
        e1=pltpu.VMEM((N, 2, B // 2), F32),
        e2=pltpu.VMEM((N, 2, B // 2), F32),
        e3=pltpu.VMEM((2 * X, 2, B // 2), F32),
        own_k=upright, own_v=upright,
        gain=pltpu.VMEM((1, W), F32),
        pair_row=pltpu.VMEM((1, N), jnp.int32),
        inverse_row=pltpu.VMEM((1, N), jnp.int32),
        pairing=pltpu.SMEM((1, N), jnp.int32),
        inverse=pltpu.SMEM((1, N), jnp.int32),
        load_sem=pltpu.SemaphoreType.DMA((4 * X + 4,)),
        send_sem=pltpu.SemaphoreType.DMA((HEAD,)),
        recv_sem=pltpu.SemaphoreType.DMA((HEAD + 2 * X,)),
    )


def body(sizes, q_in, k_in, v_in, c_in, gain_in, pairing_in, mixed_out, gq_out, gk_out, gv_out, *refs):
    s = types.SimpleNamespace(**dict(zip(scratch(sizes), refs)))
    Z, X, G = sizes
    N = Z * X
    B = Z * ROWS
    half = B // 2
    factor = 1.0 / math.sqrt(HD)
    features = float(G * X * HD)
    ctx = lax.axis_index("ctx")
    hd = lax.axis_index("head")
    z = ctx // X
    x = lax.rem(ctx, X)

    def wrap(i, n):
        return jnp.where(i >= n, i - n, i)

    after = wrap(ctx + 1, N)
    before = wrap(ctx + N - 1, N)
    over = wrap(z + 1, Z) * X
    under = wrap(z + Z - 1, Z) * X + X - 1
    columns = [wrap(x + n, X) for n in range(X)]

    def via(h, zj):
        return zj * X + 2 * lax.rem(h, 2) + lax.rem(zj + h // 2, 2)

    my_head = 2 * lax.rem(x + z, 2) + x // 2
    mine = my_head * Z + z

    def lanes(h):
        return pl.ds(pl.multiple_of(h * HD, HD), HD)

    def head_rows(h):
        return pl.ds(pl.multiple_of(h * Z, Z), Z)

    def block(ref, h):
        return ref[head_rows(h)].reshape(B, HD)

    def remote(src, dst, n, j, g, m=None):
        return pltpu.make_async_remote_copy(
            src_ref=src,
            dst_ref=dst,
            send_sem=s.send_sem.at[n],
            recv_sem=s.recv_sem.at[n if m is None else m],
            device_id=(j, g),
            device_id_type=MESH,
        )

    def loop(lo, hi, f):
        def step(k, carry):
            f(k)
            return carry

        lax.fori_loop(lo, hi, step, 0)

    def each_peer(f):
        for n in range(1, X):
            f(z * X + columns[n])

        def along_z(k):
            zj = wrap(z + k, Z)
            for n in range(X):
                f(zj * X + columns[n])

        loop(1, Z, along_z)

    def each_head_peer(f):
        loop(1, G, lambda k: f(wrap(hd + k, G)))

    def await_bytes(ref, sem):
        pltpu.make_async_copy(ref, ref, sem).wait()

    barrier = pltpu.get_barrier_semaphore()
    each_peer(lambda j: pl.semaphore_signal(barrier, inc=1, device_id=(j, hd), device_id_type=MESH))
    each_head_peer(lambda g: pl.semaphore_signal(barrier, inc=1, device_id=(ctx, g), device_id_type=MESH))

    small = (
        pltpu.make_async_copy(pairing_in, s.pair_row, s.load_sem.at[4 * X + 1]),
        pltpu.make_async_copy(pairing_in, s.pairing, s.load_sem.at[4 * X + 2]),
        pltpu.make_async_copy(gain_in, s.gain, s.load_sem.at[4 * X]),
    )
    loads = []
    for n, (src, dst) in enumerate(((k_in, s.kh), (v_in, s.vh), (q_in, s.qh), (c_in, s.ch))):
        for h in range(X):
            loads.append(
                pltpu.make_async_copy(
                    src.at[:, :, pl.ds(h * HD, HD)], dst.at[pl.ds(h * Z, Z)], s.load_sem.at[n * X + h]
                )
            )
    for copy in loads[:X] + list(small) + loads[X:]:
        copy.start()
    for copy in loads[:X]:
        copy.wait()
    s.k1[ctx] = s.kh[mine]
    pl.semaphore_wait(barrier, N - 1 + G - 1)

    def pass_on(src, relay, dst, n, edge, step, target):
        @pl.when(x != edge)
        def _():
            remote(src, dst, n, target, hd).start()

        @pl.when(x == edge)
        def _():
            for h in range(1, X):
                by = edge + h * step
                part = pl.ds(by * Z, Z)
                remote(src.at[part], relay, n, z * X + by, hd, n + 2).start()
            part = pl.ds(edge * Z, Z)
            remote(src.at[part], dst.at[part], n, target, hd).start()

    def relay_on(relay, dst, n, edge, target):
        @pl.when(x != edge)
        def _():
            await_bytes(relay, s.recv_sem.at[n + 2])
            remote(relay, dst.at[head_rows(x)], n + 2, target, hd, n).start()

    def end_pass(src, relay, n, edge):
        await_bytes(src, s.send_sem.at[n])

        @pl.when(x != edge)
        def _():
            await_bytes(relay, s.send_sem.at[n + 2])

    def spread_head(src, dst, n, h):
        def to(k):
            zj = wrap(z + k, Z)
            j = via(h, zj)

            @pl.when(j != ctx)
            def _():
                remote(src.at[h * Z + zj], dst.at[ctx], n, j, hd).start()

        loop(0, Z, to)

    def spread(src, dst, n):
        loop(0, X, lambda h: spread_head(src, dst, n, h))

    def choose(dst, src, table):
        def f(j):
            dst[j] = src[table[0, j]]

        loop(0, N, f)

    def forward(src, dst, n):
        dst[mine] = src[ctx]
        each_peer(lambda j: remote(src.at[j], dst.at[mine], n, j, hd).start())

    def await_pieces(dst, n):
        await_bytes(dst.at[pl.ds(0, N - 1)], s.recv_sem.at[n])

    spread(s.kh, s.k1, K_ONE)
    pass_on(s.kh, s.rk, s.pk, PASS_K, X - 1, -1, after)
    for copy in loads[X : 2 * X]:
        copy.wait()
    s.v1[ctx] = s.vh[mine]
    spread(s.vh, s.v1, V_ONE)
    pass_on(s.vh, s.rv, s.pv, PASS_V, X - 1, -1, after)

    for copy in list(small) + loads[2 * X :]:
        copy.wait()
    s.q1[ctx] = s.qh[mine]
    down = lax.broadcasted_iota(jnp.int32, (N, N), 0)
    across = lax.broadcasted_iota(jnp.int32, (N, N), 1)
    partners = jnp.broadcast_to(s.pair_row[...], (N, N))
    partner_of = jnp.sum(jnp.where(down == across, partners, 0), axis=1, keepdims=True)
    s.inverse_row[...] = jnp.max(jnp.where(partner_of == across, down, 0), axis=0, keepdims=True)
    turn = pltpu.make_async_copy(s.inverse_row, s.inverse, s.load_sem.at[4 * X + 3])
    turn.start()

    def own_scores(h):
        score = mm(block(s.kh, h), block(s.qh, h), 1, 1) * factor
        key_at = lax.broadcasted_iota(jnp.int32, (B, B), 0)
        query_at = lax.broadcasted_iota(jnp.int32, (B, B), 1)
        s.win[h, pl.ds(B, B)] = jnp.where(key_at <= query_at, score, -jnp.inf)
        s.gin[h] = (block(s.ch, h).astype(F32) * s.gain[:, lanes(h)]).T

    loop(0, X, own_scores)
    turn.wait()

    await_pieces(s.k1, K_ONE)
    choose(s.k2, s.k1, s.pairing)
    forward(s.k2, s.k3, K_TWO)
    relay_on(s.rk, s.pk, PASS_K, X - 1, over)
    await_pieces(s.v1, V_ONE)
    choose(s.v2, s.v1, s.pairing)
    each_peer(lambda j: remote(s.v2.at[j], s.v3.at[mine], V_TWO, j, hd, HEAD + X + my_head).start())
    pltpu.make_async_copy(s.v2.at[ctx], s.v3.at[mine], s.recv_sem.at[HEAD + X + my_head]).start()
    relay_on(s.rv, s.pv, PASS_V, X - 1, over)
    spread(s.qh, s.q1, Q_ONE)

    await_bytes(s.pk, s.recv_sem.at[PASS_K])

    def prior_scores(h):
        score = mm(block(s.pk, h), block(s.qh, h), 1, 1) * factor
        s.win[h, pl.ds(0, B)] = jnp.where(ctx > 0, score, -jnp.inf)

    loop(0, X, prior_scores)
    await_bytes(s.pv, s.recv_sem.at[PASS_V])
    await_pieces(s.k3, K_TWO)

    def softmax(h):
        s.win[h, pl.ds(2 * B, B)] = mm(block(s.k3, h), block(s.qh, h), 1, 1) * factor
        score = s.win[h]
        highest = jnp.max(score, axis=0, keepdims=True)
        logsum = highest + jnp.log(jnp.sum(jnp.exp(score - highest), axis=0, keepdims=True))
        s.lse[h] = logsum
        w = jnp.exp(score - logsum)
        s.win[h] = w
        p = w.astype(BF16)
        s.probs[h] = p
        s.acc[h] = mm(block(s.pv, h), p[0:B], 0, 0) + mm(block(s.vh, h), p[B : 2 * B], 0, 0)

    loop(0, X, softmax)
    s.stats[hd] = jnp.zeros((2, B), F32)

    def attend(h):
        await_bytes(s.v3.at[head_rows(h)], s.recv_sem.at[HEAD + X + h])
        o = s.acc[h] + mm(block(s.v3, h), s.probs[h, pl.ds(2 * B, B)], 0, 0)
        a = o.astype(BF16).astype(F32)
        s.att[h] = a
        s.stats[hd, 0:1] += jnp.sum(a * a, axis=0, keepdims=True)
        s.stats[hd, 1:2] += jnp.sum(s.gin[h] * a, axis=0, keepdims=True)

    loop(0, X, attend)
    each_head_peer(lambda g: remote(s.stats.at[hd], s.stats.at[hd], STATS, ctx, g).start())
    await_bytes(s.stats.at[pl.ds(0, G - 1)], s.recv_sem.at[STATS])
    total = jnp.sum(s.stats[...], axis=0)
    rms = lax.rsqrt(total[0:1] / features + EPSILON)
    slope = rms * rms * rms * (total[1:2] / features)

    def attn_grad(h):
        a = s.att[h]
        d = rms * s.gin[h] - a * slope
        low = d.astype(BF16)
        s.dat[h] = low
        s.d0[head_rows(h)] = d.T.astype(BF16).reshape(Z, ROWS, HD)
        spread_head(s.d0, s.d1, D_ONE, h)
        delta = jnp.sum(low.astype(F32) * a, axis=0, keepdims=True)
        s.delta[h] = delta
        logsum = s.lse[h]
        for t in range(2):
            cut = slice(t * half, (t + 1) * half)
            s.e0[2 * h + t, 0:1] = logsum[:, cut]
            s.e0[2 * h + t, 1:2] = delta[:, cut]

    loop(0, X, attn_grad)

    rows = 2 * X
    gap = (N - 1) // (rows - 1)
    row = ctx // gap
    carries = ctx == row * gap
    for r in range(rows):

        @pl.when(ctx != r * gap)
        def _():
            remote(s.e0.at[r], s.e1.at[ctx], E_ONE, r * gap, hd).start()

        @pl.when(ctx == r * gap)
        def _():
            pltpu.make_async_copy(s.e0.at[r], s.e1.at[ctx], s.recv_sem.at[E_ONE]).start()

    s.d1[ctx] = s.d0[mine]

    await_pieces(s.q1, Q_ONE)
    choose(s.q2, s.q1, s.inverse)
    forward(s.q2, s.q3, Q_TWO)

    def score_grad(h, g, values):
        dp = mm(values, s.dat[h], 1, 0)
        d = (s.win[h, pl.ds(g * B, B)] * (dp - s.delta[h])).astype(BF16)
        s.dsc[h, pl.ds(g * B, B)] = d
        return d

    def prior_terms(h):
        d = score_grad(h, 0, block(s.pv, h))
        term = (mm(d, block(s.qh, h), 1, 0) * factor).astype(BF16)
        s.bk[head_rows(h)] = term.reshape(Z, ROWS, HD)
        term = mm(s.probs[h, pl.ds(0, B)], s.dat[h], 1, 1).astype(BF16)
        s.bv[head_rows(h)] = term.reshape(Z, ROWS, HD)

    loop(0, X, prior_terms)
    pass_on(s.bv, s.rbv, s.nv, BACK_V, 0, 1, before)
    pass_on(s.bk, s.rbk, s.nk, BACK_K, 0, 1, before)

    @pl.when(carries)
    def _():
        await_bytes(s.e1, s.recv_sem.at[E_ONE])
        choose(s.e2, s.e1, s.inverse)
        each_peer(lambda j: remote(s.e2.at[j], s.e3.at[row], E_TWO, j, hd).start())
        pltpu.make_async_copy(s.e2.at[ctx], s.e3.at[row], s.recv_sem.at[E_TWO]).start()

    def own_terms(h):
        d = score_grad(h, 1, block(s.vh, h))
        s.own_k[h] = mm(d, block(s.qh, h), 1, 0) * factor
        s.own_v[h] = mm(s.probs[h, pl.ds(B, B)], s.dat[h], 1, 1)

    loop(0, X, own_terms)

    await_pieces(s.d1, D_ONE)
    choose(s.d2, s.d1, s.inverse)
    each_peer(lambda j: remote(s.d2.at[j], s.d3.at[mine], D_TWO, j, hd, HEAD + my_head).start())
    pltpu.make_async_copy(s.d2.at[ctx], s.d3.at[mine], s.recv_sem.at[HEAD + my_head]).start()
    relay_on(s.rbv, s.nv, BACK_V, 0, under)
    relay_on(s.rbk, s.nk, BACK_K, 0, under)

    def query_terms(h):
        d = score_grad(h, 2, block(s.v3, h))
        gq = (
            mm(s.dsc[h, pl.ds(0, B)], block(s.pk, h), 0, 0)
            + mm(s.dsc[h, pl.ds(B, B)], block(s.kh, h), 0, 0)
            + mm(d, block(s.k3, h), 0, 0)
        )
        gq_out[:, lanes(h)] = (gq * factor).astype(BF16)
        mixed_out[:, lanes(h)] = ((s.att[h] * rms).T * s.gain[:, lanes(h)]).astype(BF16)

    loop(0, X, query_terms)

    await_pieces(s.q3, Q_TWO)
    await_bytes(s.e3, s.recv_sem.at[E_TWO])

    def incoming(h, n):
        return jnp.concatenate([s.e3[2 * h, n : n + 1], s.e3[2 * h + 1, n : n + 1]], axis=1)

    def incoming_probs(h):
        w = jnp.exp(mm(block(s.kh, h), block(s.q3, h), 1, 1) * factor - incoming(h, 0))
        s.win_in[h] = w
        s.probs_in[h] = w.astype(BF16)

    loop(0, X, incoming_probs)
    await_bytes(s.nv, s.recv_sem.at[BACK_V])
    await_bytes(s.nk, s.recv_sem.at[BACK_K])

    def add_next(h):
        s.own_v[h] += block(s.nv, h).astype(F32)
        s.own_k[h] += block(s.nk, h).astype(F32)

    loop(0, X, add_next)

    def partner_terms(h):
        await_bytes(s.d3.at[head_rows(h)], s.recv_sem.at[HEAD + h])
        d = block(s.d3, h)
        gv_out[:, lanes(h)] = (s.own_v[h] + mm(s.probs_in[h], d, 1, 0)).astype(BF16)
        dp = mm(block(s.vh, h), d, 1, 1)
        ds = (s.win_in[h] * (dp - incoming(h, 1))).astype(BF16)
        gk_out[:, lanes(h)] = (s.own_k[h] + mm(ds, block(s.q3, h), 1, 0) * factor).astype(BF16)

    loop(0, X, partner_terms)

    for n in (K_ONE, V_ONE, Q_ONE, D_ONE, K_TWO, V_TWO, Q_TWO, D_TWO):
        await_bytes(s.k1.at[pl.ds(0, N - 1)], s.send_sem.at[n])
    await_bytes(s.stats.at[pl.ds(0, G - 1)], s.send_sem.at[STATS])
    end_pass(s.kh, s.rk, PASS_K, X - 1)
    end_pass(s.vh, s.rv, PASS_V, X - 1)
    end_pass(s.bv, s.rbv, BACK_V, 0)
    end_pass(s.bk, s.rbk, BACK_K, 0)

    @pl.when(carries)
    def _():
        await_bytes(s.e0.at[pl.ds(0, rows - 1)], s.send_sem.at[E_ONE])
        await_bytes(s.e2.at[pl.ds(0, N - 1)], s.send_sem.at[E_TWO])

    @pl.when(jnp.logical_not(carries))
    def _():
        await_bytes(s.e0, s.send_sem.at[E_ONE])


def write_out(*refs):
    sem = refs[8]
    copies = [pltpu.make_async_copy(refs[n], refs[4 + n], sem.at[n]) for n in range(4)]
    for copy in copies:
        copy.start()
    for copy in copies:
        copy.wait()


def on_device(sizes, queries, key_rows, value_rows, cotangent, norm_gain, pairing):
    Z, X, G = sizes
    N, B, W = Z * X, Z * ROWS, X * HD
    tiles = (Z, ROWS, W)
    hbm = pl.BlockSpec(memory_space=pltpu.HBM)
    out = jax.ShapeDtypeStruct((B, W), BF16)
    held = pl.pallas_call(
        functools.partial(body, sizes),
        out_shape=(pltpu.VMEM((B, W), BF16),) * 4,
        in_specs=[hbm] * 6,
        out_specs=(pl.BlockSpec(memory_space=pltpu.VMEM),) * 4,
        scratch_shapes=list(scratch(sizes).values()),
        compiler_params=pltpu.CompilerParams(
            collective_id=0, has_side_effects=True, vmem_limit_bytes=56 << 20
        ),
    )(
        queries.reshape(tiles),
        key_rows.reshape(tiles),
        value_rows.reshape(tiles),
        cotangent.reshape(tiles),
        norm_gain.reshape(1, W),
        pairing.reshape(1, N),
    )
    return pl.pallas_call(
        write_out,
        out_shape=(out,) * 4,
        in_specs=[pl.BlockSpec(memory_space=pltpu.VMEM)] * 4,
        out_specs=(hbm,) * 4,
        scratch_shapes=[pltpu.SemaphoreType.DMA((4,))],
        compiler_params=pltpu.CompilerParams(vmem_limit_bytes=4 << 20),
    )(*held)


def solution(mesh):
    heads_here = 4
    sizes = (mesh.shape["ctx"] // heads_here, heads_here, mesh.shape["head"])
    spec = P("ctx", "head")
    return jax.shard_map(
        functools.partial(on_device, sizes),
        mesh=mesh,
        in_specs=(spec, spec, spec, spec, P("head"), P()),
        out_specs=(spec,) * 4,
        check_vma=False,
    )
```
